256 devices in a mesh: dp: 16 (over y, x_hi, core), tensor: 16 (over x_lo, z).
Axes of the slice: x: 4 (x_hi: 2, x_lo: 2; x = x_hi * 2 + x_lo), y: 4, z: 8, core: 2. Of those that a mesh axis runs over, the one named last changes fastest.
Arguments:
- acts: bfloat16 [32, 256, 36864], P('dp', None, 'tensor'), may hold values from -18 to 18
- out_grads: bfloat16 [32, 256, 4608], P('dp', None, 'tensor'), may hold values from -0.000115088994 to 0.000115088994
- other_sq: float32 [32, 128], P('dp', 'tensor'), may hold values from 0.00390625 to 0.2109375
- noise: float32 [4608, 36864], P('dp', 'tensor'), may hold values from -6 to 6
Outputs:
- noisy_grad: float32 [4608, 36864], P('dp', 'tensor')
The draws below stay inside these ranges and needn't reach their ends.
All inputs are finite; a program needn't handle non-finite values.
Results may differ from the reference program's by a relative error of at most 0.019.
Values may be sent and summed in bfloat16 or wider, within the bound.
No kernel may reach another device: no remote copies, remote signals or barrier semaphores. Data moves between devices by JAX's collectives and lax.ppermute only.
A program may use at most 192 MiB of HBM per device.

```python
import math
import jax
import jax.numpy as jnp
from jax import lax

D = 4608
FF = 36864
T_SIZE = 256
EXAMPLES = 32
OTHER = 128


def permute_tokens(example_key):
    return jax.random.permutation(example_key, T_SIZE)


def token_pairs(key):
    pair_key = jax.random.fold_in(key, 5)
    example_keys = jax.random.split(pair_key, EXAMPLES)
    return jax.vmap(permute_tokens)(example_keys)


def mix_tokens(values, partner):
    moved = jnp.take_along_axis(values, partner[:, :, None], axis=1)
    return 0.8 * values + 0.6 * moved


def draw_acts(key, part):
    partner = token_pairs(key)
    key = jax.random.fold_in(key, 11)
    k_val, k_col = jax.random.split(key, 2)
    columns = jnp.arange(FF, dtype=jnp.float32) / FF
    col_scale = 3.0 ** columns * jax.random.uniform(k_col, (FF,), jnp.float32, 0.5, 1.5)
    values = jax.random.normal(k_val, (EXAMPLES, T_SIZE, FF), jnp.float32)
    values = mix_tokens(values, partner)
    values = jnp.clip(values, -4.0, 4.0) * col_scale
    return values.astype(jnp.bfloat16)


def draw_out_grads(key, part):
    partner = token_pairs(key)
    key = jax.random.fold_in(key, 23)
    k_val, k_col, k_perm, k_off = jax.random.split(key, 4)
    order = jax.random.permutation(k_perm, EXAMPLES).astype(jnp.float32)
    offset = jax.random.uniform(k_off, (EXAMPLES,), jnp.float32, 0.0, 1.0)
    example_scale = 0.1 * 40.0 ** ((order + offset) / EXAMPLES)
    col_scale = jax.random.uniform(k_col, (D,), jnp.float32, 0.5, 1.5)
    values = jax.random.normal(k_val, (EXAMPLES, T_SIZE, D), jnp.float32)
    values = mix_tokens(values, partner)
    values = jnp.clip(values, -4.0, 4.0) * col_scale * example_scale[:, None, None]
    values = values * (T_SIZE * FF * D) ** (-0.5)
    return values.astype(jnp.bfloat16)


def draw_other_sq(key, part):
    key = jax.random.fold_in(key, 37)
    k_ex, k_val = jax.random.split(key, 2)
    example_scale = jnp.exp(jax.random.uniform(k_ex, (EXAMPLES, 1), jnp.float32, 0.0, math.log(6.0))) / OTHER
    columns = jnp.arange(OTHER, dtype=jnp.float32) / max(OTHER - 1, 1)
    rising = 1.0 + 2.0 * columns
    entry = jnp.exp(jax.random.uniform(k_val, (EXAMPLES, OTHER), jnp.float32, math.log(0.5), math.log(1.5)))
    values = example_scale * rising[None, :] * entry
    return values.astype(jnp.float32)


def level_of(key, extent, cuts, low, largest):
    loudness, own = 1.0, jax.random.fold_in(key, 6)
    for dim, parts in cuts:
        steps = jnp.exp(jax.random.uniform(jax.random.fold_in(own, dim), (parts,), jnp.float32, low / len(cuts), largest / len(cuts)))
        loudness = loudness * jnp.repeat(steps, extent[dim] // parts).reshape([-1 if axis == dim else 1 for axis in range(len(extent))])
    return loudness


def centred(key, dims, spread, most, cuts=(), kind=jnp.bfloat16):
    array = spread * jax.random.normal(key, dims, jnp.float32)
    if cuts:
        array = array * level_of(key, dims, cuts, -0.22, 0.18)
    return jnp.clip(array, -most, most).astype(kind)


def setup_inputs(seed: int = 0) -> dict:
    arg_keys = jax.random.split(jax.random.key(seed), 5)
    return {
        "acts": draw_acts(jax.random.fold_in(arg_keys[4], 71), 0),
        "out_grads": draw_out_grads(jax.random.fold_in(arg_keys[4], 71), 0),
        "other_sq": draw_other_sq(jax.random.fold_in(arg_keys[4], 71), 0),
        "noise": centred(arg_keys[3], (D, FF), 1.0, 6.0, ((0, 16), (1, 16)), jnp.float32),
    }


clip_norm = 2.5

def reference(acts, out_grads, other_sq, noise):

    def norm_one(pair):
        act_b, grad_b = pair
        act_gram = jnp.dot(act_b, act_b.T, preferred_element_type=jnp.float32)
        grad_gram = jnp.dot(grad_b, grad_b.T, preferred_element_type=jnp.float32)
        return jnp.sum(act_gram * grad_gram)
    squares = lax.map(norm_one, (acts, out_grads))
    total = squares + lax.optimization_barrier(jnp.sum(other_sq, axis=1))
    clip = jnp.minimum(1.0, clip_norm / jnp.sqrt(total))

    def add_one(carry, item):
        act_b, grad_b, clip_b = item
        scaled = (clip_b * grad_b.astype(jnp.float32)).astype(jnp.bfloat16)
        term = jnp.dot(scaled.T, act_b, preferred_element_type=jnp.float32).astype(jnp.bfloat16)
        term = lax.optimization_barrier(term)
        return (carry + term.astype(jnp.float32), None)
    zeros = jnp.zeros((D, FF), jnp.float32)
    summed, _ = lax.scan(add_one, zeros, (acts, out_grads, clip))
    factor = math.sqrt(FF * D) / clip_norm
    return (factor * summed + noise) / math.sqrt(EXAMPLES)
```

```python
import functools
import math

import jax
import jax.numpy as jnp
from jax import lax
from jax.experimental import pallas as pl
from jax.experimental.pallas import tpu as pltpu
from jax.sharding import PartitionSpec as P

clip_norm = 2.5
AXES = ("dp", "tensor")
NY, NX, NZ = 4, 4, 8
OFF = (0, 1, 2, -1)
BF = jnp.bfloat16
F32 = jnp.float32


def coords(i):
    dp, te = divmod(i, 2 * NZ)
    return dp // 4, (dp // 2) % 2, dp % 2, te // NZ, te % NZ


def index(y, xh, c, xl, z):
    return ((y % NY * 2 + xh) * 2 + c) * 2 * NZ + xl * NZ + z % NZ


def perm_of(move):
    return [(i, index(*move(*coords(i)))) for i in range(NY * NX * NZ * 2)]


def along_x(step):
    def move(y, xh, c, xl, z):
        x = (xh * 2 + xl + step) % NX
        return y, x // 2, c, x % 2, z

    return perm_of(move)


def along_y(step):
    return perm_of(lambda y, xh, c, xl, z: (y + step, xh, c, xl, z))


def along_z(step):
    return perm_of(lambda y, xh, c, xl, z: (y, xh, c, xl, z + step))


def flip_z(bit):
    return perm_of(lambda y, xh, c, xl, z: (y, xh, c, xl, z ^ bit))


def spread(flip):
    def move(y, xh, c, xl, z):
        t, u = (z // 2) % 2, z % 2
        m = 2 * (xh ^ t) + (c ^ u)
        return y, t, u, xl ^ flip, z + OFF[m]

    return perm_of(move)


CORE = perm_of(lambda y, xh, c, xl, z: (y, xh, 1 - c, xl, z))
XHI = perm_of(lambda y, xh, c, xl, z: (y, 1 - xh, c, xl, z))
XLO = perm_of(lambda y, xh, c, xl, z: (y, xh, c, 1 - xl, z))


def send(value, perm):
    return lax.ppermute(value, AXES, perm)


SLOTS = (2, 1, 3, 0)


def scale_kernel(place_ref, clip_ref, *refs):
    pieces, out_ref = refs[:-1], refs[-1]
    blocks = []
    for ref in pieces:
        blocks += [ref.at[0], ref.at[1]]
    half = out_ref.shape[3] // 2
    for i, block in enumerate(blocks):
        slot, m = place_ref[2 * i], place_ref[2 * i + 1]
        for e in range(2):
            cols = slice(e * half, (e + 1) * half)
            out_ref[slot, m, :, cols] = (
                clip_ref[2 * m + e] * block[:, cols].astype(F32)
            ).astype(BF)


def scale_grads(places, clips, pieces):
    _, rows, tokens = pieces[0].shape
    smem = pl.BlockSpec(memory_space=pltpu.SMEM)
    vmem = pl.BlockSpec(memory_space=pltpu.VMEM)
    return pl.pallas_call(
        scale_kernel,
        out_shape=jax.ShapeDtypeStruct((4, 4, rows, tokens), BF),
        in_specs=[smem, smem] + [vmem] * len(pieces),
        out_specs=vmem,
        cost_estimate=pl.CostEstimate(
            flops=16 * rows * tokens, bytes_accessed=64 * rows * tokens, transcendentals=0
        ),
        compiler_params=pltpu.CompilerParams(vmem_limit_bytes=40 * 1024 * 1024),
        name="scale_grads",
    )(places, clips, *pieces)


def product_kernel(s_ref, *refs):
    acts, outs = refs[:6], refs[6:]
    slots, _, rows, tokens = s_ref.shape
    j, steps = pl.program_id(0), pl.num_programs(0)
    total = None
    first = 0
    for a_ref in acts:
        count = a_ref.shape[0]
        m, start = first // tokens, first % tokens
        left = s_ref[:, m, :, start : start + count].reshape(slots * rows, count)
        part = jnp.dot(left, a_ref[...], preferred_element_type=F32)
        total = part if total is None else total + part
        first += count
    total = total.astype(outs[0].dtype)
    if len(outs) == 1:
        outs[0][...] = total
        return

    @pl.when(j < steps // 2)
    def _():
        for slot in range(slots):
            outs[2 * slot][...] = total[slot * rows : (slot + 1) * rows]

    @pl.when(j >= steps // 2)
    def _():
        for slot in range(slots):
            outs[2 * slot + 1][...] = total[slot * rows : (slot + 1) * rows]


def product(scaled, first, slots, acts, tile, split):
    _, quarters, rows, tokens = scaled.shape
    width = acts[0].shape[1]
    steps = width // tile
    if split:
        out_shape = [jax.ShapeDtypeStruct((rows, width // 2), BF)] * (2 * slots)
        low = pl.BlockSpec((rows, tile), lambda j: (0, jnp.minimum(j, steps // 2 - 1)))
        high = pl.BlockSpec((rows, tile), lambda j: (0, jnp.maximum(j - steps // 2, 0)))
        out_specs = [low, high] * slots
    else:
        out_shape = [jax.ShapeDtypeStruct((rows, width), F32)]
        out_specs = [pl.BlockSpec((rows, tile), lambda j: (0, j))]
    depth = quarters * tokens
    return pl.pallas_call(
        product_kernel,
        out_shape=out_shape,
        grid=(steps,),
        in_specs=[
            pl.BlockSpec((slots, quarters, rows, tokens), lambda j: (first // slots, 0, 0, 0))
        ]
        + [pl.BlockSpec((a.shape[0], tile), lambda j: (0, j)) for a in acts],
        out_specs=out_specs,
        cost_estimate=pl.CostEstimate(
            flops=2 * slots * rows * depth * width,
            bytes_accessed=2 * (slots * rows * depth + depth * width + slots * rows * width),
            transcendentals=0,
        ),
        compiler_params=pltpu.CompilerParams(vmem_limit_bytes=40 * 1024 * 1024),
        name=f"product_{first}",
    )(scaled, *acts)


def halved(grams, bit, perm):
    low, high = jnp.split(grams, 2, axis=1)
    keep, give = jnp.where(bit == 0, low, high), jnp.where(bit == 0, high, low)
    return (keep.astype(F32) + send(give, perm).astype(F32)).astype(BF)


def shards(acts, out_grads, other_sq, noise):
    dp, te = lax.axis_index("dp"), lax.axis_index("tensor")
    y, xh, c, xl, z = dp // 4, (dp // 2) % 2, dp % 2, te // NZ, te % NZ
    examples, seq, columns = acts.shape
    tokens = examples * seq
    features = out_grads.shape[2]
    half = columns // 2
    stage = lax.optimization_barrier

    flat = acts.reshape(tokens, columns)
    up = send(flat[:seq], along_x(1))
    down = send(flat[seq:], along_x(-1))
    grads_t = out_grads.reshape(tokens, features).T
    own = jnp.stack([send(grads_t, spread(0)), send(grads_t, spread(1))])
    fwd, bwd = [own], [own]
    fwd.append(send(own, along_z(1)))
    bwd.append(send(own, along_z(-1)))
    act_gram = jnp.einsum("btf,bsf->bts", acts, acts, preferred_element_type=F32)
    grad_gram = jnp.einsum("btf,bsf->bts", out_grads, out_grads, preferred_element_type=F32)
    grams = jnp.concatenate([act_gram, grad_gram]).astype(BF)
    grams = halved(grams, xl, XLO)
    grams = halved(grams, z // 4, flip_z(4))
    grams = halved(grams, (z // 2) % 2, flip_z(2))
    up, down, fwd[1], bwd[1], grams = stage((up, down, fwd[1], bwd[1], grams))

    up, down = send(up, along_x(1)), send(down, along_x(-1))
    sibling = send(flat, CORE)
    for _ in range(2):
        fwd.append(send(fwd[-1], along_z(1)))
        bwd.append(send(bwd[-1], along_z(-1)))
    grams = halved(grams, z % 2, flip_z(1)).astype(F32)
    total = jnp.sum(grams[:examples] * grams[examples:], axis=(1, 2)) + jnp.sum(other_sq, axis=1)
    total = total + send(total, flip_z(1))
    total = total + send(total, flip_z(2))
    up, down, fwd[3], bwd[3], total = stage((up, down, fwd[3], bwd[3], total))

    far = [send(fwd[3][0], along_z(1)), send(bwd[3][1], along_z(-1))]
    up_sibling, down_sibling = send(up, CORE), send(down, CORE)
    total = total + send(total, flip_z(4))
    total = total + send(total, XLO)
    far[0], far[1], total = stage((far[0], far[1], total))
    far = jnp.stack(far)
    clip = jnp.minimum(1.0, clip_norm / jnp.sqrt(total))
    clips = jnp.concatenate([clip, send(clip, CORE)])
    clips = jnp.concatenate([clips, send(clips, XHI)])

    pieces = [own, fwd[1], fwd[2], fwd[3], far, bwd[3], bwd[2], bwd[1]]
    places = []
    for r in range(NZ):
        q = (z - r - 2 * xh - c) % NZ
        m = jnp.where(q % 4 == 3, 3, q % 4)
        k = jnp.where(q % 4 == 3, (q // 4 + 1) % 2, q // 4)
        for f in range(2):
            step = (2 * (f ^ xl) + k - y) % 4
            slot = jnp.where(step == 2, 0, jnp.where(step == 0, 3, jnp.where(step == 1, 1, 2)))
            places += [slot, m]
    places = jnp.stack(places).astype(jnp.int32)
    scaled = scale_grads(places, clips, pieces)

    held = [flat, sibling, up, down, up_sibling, down_sibling]
    tile = columns // 6
    far_a, far_b = product(scaled, 0, 1, held, tile, True)
    from_down, from_up = send(far_a, along_y(1)), send(far_b, along_y(-1))
    (next_a, next_b), (prev_a, prev_b) = [
        product(scaled, slot, 1, held, tile, True) for slot in (1, 2)
    ]
    next_b, prev_a = send(next_b, along_y(1)), send(prev_a, along_y(-1))
    next_a = send((next_a.astype(F32) + from_down.astype(F32)).astype(BF), along_y(1))
    prev_b = send((prev_b.astype(F32) + from_up.astype(F32)).astype(BF), along_y(-1))
    (mine,) = product(scaled, 3, 1, held, tile, False)

    width = features * 2 * NZ
    factor = math.sqrt(columns * 2 * NZ * width) / clip_norm
    base = factor * mine + noise
    summed = jnp.concatenate(
        [next_a.astype(F32) + prev_a.astype(F32), next_b.astype(F32) + prev_b.astype(F32)], axis=1
    )
    return (base + factor * summed) / math.sqrt(examples * 4 * NY)


def solution(mesh):
    placed = (
        P("dp", None, "tensor"),
        P("dp", None, "tensor"),
        P("dp", "tensor"),
        P("dp", "tensor"),
    )
    return jax.shard_map(
        shards, mesh=mesh, in_specs=placed, out_specs=P("dp", "tensor"), check_vma=False
    )
```

```python
import functools
import math

import jax
import jax.numpy as jnp
from jax import lax
from jax.experimental import pallas as pl
from jax.experimental.pallas import tpu as pltpu
from jax.sharding import PartitionSpec as P

clip_norm = 2.5
AXES = ("dp", "tensor")
NY, NX, NZ = 4, 4, 8
STEP_Z = ((4, -3), (-1, 2), (0, 1), (-2, 3))
MEMBER = [0] * NZ
for away in range(NY):
    for other in range(2):
        MEMBER[STEP_Z[away][other] % NZ] = 2 * away + other
BF = jnp.bfloat16
F32 = jnp.float32


def coords(i):
    dp, te = divmod(i, 2 * NZ)
    return dp // 4, (dp // 2) % 2, dp % 2, te // NZ, te % NZ


def index(y, xh, c, xl, z):
    return ((y % NY * 2 + xh) * 2 + c) * 2 * NZ + xl * NZ + z % NZ


def perm_of(move):
    return [(i, index(*move(*coords(i)))) for i in range(NY * NX * NZ * 2)]


def along_x(step):
    def move(y, xh, c, xl, z):
        x = (xh * 2 + xl + step) % NX
        return y, x // 2, c, x % 2, z

    return perm_of(move)


def along_y(step):
    return perm_of(lambda y, xh, c, xl, z: (y + step, xh, c, xl, z))


def along_z(step):
    return perm_of(lambda y, xh, c, xl, z: (y, xh, c, xl, z + step))


def flip_z(bit):
    return perm_of(lambda y, xh, c, xl, z: (y, xh, c, xl, z ^ bit))


def spread(turn):
    def move(y, xh, c, xl, z):
        row_y, row_x, row_c = 2 * xl + z // 4, (z // 2) % 2, z % 2
        step = STEP_Z[(y - row_y) % NY][c ^ row_c]
        return row_y, xh, row_c, xl ^ row_x ^ turn, z + step

    return perm_of(move)


CORE = perm_of(lambda y, xh, c, xl, z: (y, xh, 1 - c, xl, z))
XHI = perm_of(lambda y, xh, c, xl, z: (y, 1 - xh, c, xl, z))
XLO = perm_of(lambda y, xh, c, xl, z: (y, xh, c, 1 - xl, z))


def send(value, perm):
    return lax.ppermute(value, AXES, perm)


def scale_kernel(theirs, id_ref, clip_ref, ring_ref, out_ref):
    dp = id_ref[0]
    y, xh, c = dp // 4, (dp // 2) % 2, dp % 2
    row_x = 1 - xh if theirs else xh
    source = 4 * (y % 2) + 2 * row_x + c
    half = out_ref.shape[2] // 2
    for z in range(NZ):
        m = id_ref[1 + (z - source + NZ) % NZ]
        member = 2 * ((y + m // 2) % NY) + (c + m) % 2
        for e in range(2):
            cols = slice(e * half, (e + 1) * half)
            out_ref[m, :, cols] = (
                clip_ref[2 * member + e] * ring_ref[z, :, cols].astype(F32)
            ).astype(BF)


def scale_grads(theirs, ids, clips, ring):
    _, rows, tokens = ring.shape
    smem = pl.BlockSpec(memory_space=pltpu.SMEM)
    vmem = pl.BlockSpec(memory_space=pltpu.VMEM)
    return pl.pallas_call(
        functools.partial(scale_kernel, theirs),
        out_shape=jax.ShapeDtypeStruct(ring.shape, BF),
        in_specs=[smem, smem, vmem],
        out_specs=vmem,
        cost_estimate=pl.CostEstimate(
            flops=8 * rows * tokens, bytes_accessed=32 * rows * tokens, transcendentals=0
        ),
        compiler_params=pltpu.CompilerParams(vmem_limit_bytes=24 * 1024 * 1024),
        name="scale_theirs" if theirs else "scale_mine",
    )(ids, clips, ring)


def product_kernel(s_ref, *refs):
    acts, out_ref = refs[:-1], refs[-1]
    tokens = s_ref.shape[2]
    total = None
    first = 0
    for a_ref in acts:
        count = a_ref.shape[0]
        m, start = first // tokens, first % tokens
        part = jnp.dot(s_ref[m, :, start : start + count], a_ref[...], preferred_element_type=F32)
        total = part if total is None else total + part
        first += count
    out_ref[...] = total.astype(out_ref.dtype)


def product(name, scaled, acts, width, tile, dtype):
    members, rows, tokens = scaled.shape
    depth = members * tokens

    def spec(height, first):
        return pl.BlockSpec((height, tile), lambda j: (0, j + first // tile))

    return pl.pallas_call(
        product_kernel,
        out_shape=jax.ShapeDtypeStruct((rows, width), dtype),
        grid=(width // tile,),
        in_specs=[pl.BlockSpec((members, rows, tokens), lambda j: (0, 0, 0))]
        + [spec(a.shape[0], first) for a, first in acts],
        out_specs=spec(rows, 0),
        cost_estimate=pl.CostEstimate(
            flops=2 * rows * depth * width,
            bytes_accessed=2 * (rows * depth + depth * width + rows * width),
            transcendentals=0,
        ),
        compiler_params=pltpu.CompilerParams(vmem_limit_bytes=40 * 1024 * 1024),
        name=name,
    )(scaled, *[a for a, _ in acts])


def shards(acts, out_grads, other_sq, noise):
    dp, te = lax.axis_index("dp"), lax.axis_index("tensor")
    y, xh, xl = dp // 4, (dp // 2) % 2, te // NZ
    examples, seq, columns = acts.shape
    tokens = examples * seq
    features = out_grads.shape[2]
    rows = features // 2
    tile = columns // 3
    stage = lax.optimization_barrier
    ids = jnp.stack([dp] + [jnp.int32(m) for m in MEMBER]).astype(jnp.int32)

    grads_t = out_grads.reshape(tokens, features).T
    sources = [send(grads_t, spread(0)), send(grads_t, spread(1))]

    def blocks(x):
        gram = jnp.einsum("btf,bsf->bts", x, x, preferred_element_type=F32).astype(BF)
        mid = seq // 2
        return jnp.stack([gram[:, :mid, :mid], gram[:, :mid, mid:], gram[:, mid:, mid:]])

    grams = jnp.stack([blocks(acts), blocks(out_grads)])
    flat = acts.reshape(tokens, columns)
    grams, flat = stage((grams, flat))

    def near(k):
        part = flat[:, k * tile : (k + 1) * tile]
        return send(part, along_y(1)), send(part, along_y(-1))

    below, above = near(0)
    below, above = [below], [above]
    sibling = send(flat, CORE)
    shape = grams.shape
    grams = jnp.moveaxis(grams.reshape(shape[:3] + (2 * NZ, -1, shape[4])), 3, 0)
    grams = lax.all_to_all(grams, "tensor", 0, 0, tiled=True).astype(F32).sum(axis=0)
    sources[0], sources[1], grams, flat = stage((sources[0], sources[1], grams, flat))

    turn = xl ^ (y // 2) ^ xh
    z_rings = [list(range(first, first + NZ)) for first in (0, NZ)]
    theirs, mine = [
        lax.all_gather(
            jnp.where(turn == t, sources[0], sources[1])[None],
            "tensor",
            axis=0,
            tiled=True,
            axis_index_groups=z_rings,
        )
        for t in (1, 0)
    ]
    for side, value in zip((below, above), near(1)):
        side.append(value)
    weight = jnp.array([1.0, 2.0, 1.0], F32)[:, None, None, None]
    total = jnp.sum(grams[0] * grams[1] * weight, axis=(0, 2, 3)) + jnp.sum(other_sq, axis=1)
    total = lax.all_to_all(
        jnp.broadcast_to(total, (2 * NZ, examples)), "tensor", 0, 0, tiled=True
    ).sum(axis=0)
    clip = jnp.minimum(1.0, clip_norm / jnp.sqrt(total))
    clip, below, above = stage((clip, below, above))

    far_below = send(jnp.concatenate([b[:seq] for b in below], axis=1), along_y(1))
    far_above = send(jnp.concatenate([a[seq:] for a in above], axis=1), along_y(-1))
    clip, far_below, far_above, flat = stage((clip, far_below, far_above, flat))
    columns_y = [[4 * k + 2 * x + core for k in range(NY) for core in range(2)] for x in range(2)]
    clips = lax.all_to_all(
        jnp.broadcast_to(clip, (2 * NY, examples)),
        "dp",
        0,
        0,
        tiled=True,
        axis_index_groups=columns_y,
    ).reshape(-1)
    clips, flat, far_below, far_above = stage((clips, flat, far_below, far_above))
    for side, value in zip((below, above), near(2)):
        side.append(value)

    def swap(array):
        return send(array, CORE)

    far_sibling = [swap(far_below), swap(far_above)]
    near_sibling = [(swap(above[k]), swap(below[k])) for k in range(2)]

    def held(k, far, far_other, first):
        parts = [(flat, k * tile), (sibling, k * tile), (above[k], 0), (near_sibling[k][0], 0)]
        parts += [(a, first) for a in far + far_other]
        return parts + [(below[k], 0), (near_sibling[k][1], 0)]

    scaled = scale_grads(True, ids, clips, theirs)
    early = [held(k, [far_below, far_above], far_sibling, k * tile) for k in range(2)]
    part = jnp.concatenate(
        [product(f"theirs_{k}", scaled, early[k], tile, tile, BF) for k in range(2)], axis=1
    )
    low, high = send(part[:rows], along_x(1)), send(part[rows:], along_x(-1))
    low, high, below[2], above[2] = stage((low, high, below[2], above[2]))
    low, high = send(low, along_x(1)), send(high, along_x(-1))
    far = [send(below[2][:seq], along_y(1)), send(above[2][seq:], along_y(-1))]
    near_sibling.append((swap(above[2]), swap(below[2])))
    low, high, far = stage((low, high, far))

    late = held(2, far, [swap(a) for a in far], 0)
    part = product("theirs_2", scaled, late, tile, tile, BF)
    part, mine = stage((part, mine))
    low2, high2 = send(part[:rows], along_x(1)), send(part[rows:], along_x(-1))
    scaled = scale_grads(False, ids, clips, mine)
    own = [product(f"mine_{k}", scaled, early[k], tile, tile, F32) for k in range(2)]
    low2, high2 = send(low2, along_x(1)), send(high2, along_x(-1))
    own.append(product("mine_2", scaled, late, tile, tile, F32))

    width = features * 2 * NZ
    factor = math.sqrt(columns * 2 * NZ * width) / clip_norm
    root = math.sqrt(examples * 4 * NY)
    parts = []
    for k in range(3):
        up, down = (low2, high2) if k == 2 else (low, high)
        first = 0 if k == 2 else k * tile
        got = jnp.concatenate([a[:, first : first + tile] for a in (up, down)]).astype(F32)
        parts.append((factor * (own[k] + got) + noise[:, k * tile : (k + 1) * tile]) / root)
    return jnp.concatenate(parts, axis=1)


def solution(mesh):
    placed = (
        P("dp", None, "tensor"),
        P("dp", None, "tensor"),
        P("dp", "tensor"),
        P("dp", "tensor"),
    )
    return jax.shard_map(
        shards, mesh=mesh, in_specs=placed, out_specs=P("dp", "tensor"), check_vma=False
    )
```

```python
import math

import jax
import jax.numpy as jnp
from jax import lax
from jax.experimental import pallas as pl
from jax.experimental.pallas import tpu as pltpu
from jax.sharding import PartitionSpec as P

clip_norm = 2.5
AXES = ("dp", "tensor")
NY, NX, NZ = 4, 4, 8
BF = jnp.bfloat16
F32 = jnp.float32


def coords(i):
    dp, te = divmod(i, 2 * NZ)
    return dp // 4, (dp // 2) % 2, dp % 2, te // NZ, te % NZ


def index(y, xh, c, xl, z):
    return ((y % NY * 2 + xh) * 2 + c) * 2 * NZ + xl * NZ + z % NZ


def perm_of(move):
    return [(i, index(*move(*coords(i)))) for i in range(NY * NX * NZ * 2)]


def along_x(step):
    def move(y, xh, c, xl, z):
        x = (xh * 2 + xl + step) % NX
        return y, x // 2, c, x % 2, z

    return perm_of(move)


def along_y(step):
    return perm_of(lambda y, xh, c, xl, z: (y + step, xh, c, xl, z))


def along_z(step):
    return perm_of(lambda y, xh, c, xl, z: (y, xh, c, xl, z + step))


def flip_z(bit):
    return perm_of(lambda y, xh, c, xl, z: (y, xh, c, xl, z ^ bit))


def spread(turn):
    def move(y, xh, c, xl, z):
        row_y, row_x, row_c = 2 * xl + z // 4, (z // 2) % 2, z % 2
        step = 2 * ((y - row_y) % NY) + (c ^ row_c) - 2 * row_x
        return row_y, xh, row_c, xl ^ row_x ^ turn, z + step

    inside = perm_of(lambda *at: at[:1] + move(*at)[1:])
    return inside, [(mid, end) for (_, mid), (_, end) in zip(inside, perm_of(move))]


CORE = perm_of(lambda y, xh, c, xl, z: (y, xh, 1 - c, xl, z))
XHI = perm_of(lambda y, xh, c, xl, z: (y, 1 - xh, c, xl, z))
XLO = perm_of(lambda y, xh, c, xl, z: (y, xh, c, 1 - xl, z))


def send(value, perm):
    return lax.ppermute(value, AXES, perm)


def scale_kernel(id_ref, clip_ref, ring_ref, out_ref):
    dp = id_ref[0]
    y, c = dp // 4, dp % 2
    half = out_ref.shape[2] // 2
    for z in range(NZ):
        m = (z - 4 * (y % 2) - c + NZ) % NZ
        member = 2 * ((y + m // 2) % NY) + (c + m) % 2
        for e in range(2):
            cols = slice(e * half, (e + 1) * half)
            out_ref[m, :, cols] = (
                clip_ref[2 * member + e] * ring_ref[z, :, cols].astype(F32)
            ).astype(BF)


def scale_grads(name, ids, clips, ring):
    _, rows, tokens = ring.shape
    smem = pl.BlockSpec(memory_space=pltpu.SMEM)
    vmem = pl.BlockSpec(memory_space=pltpu.VMEM)
    return pl.pallas_call(
        scale_kernel,
        out_shape=jax.ShapeDtypeStruct(ring.shape, BF),
        in_specs=[smem, smem, vmem],
        out_specs=vmem,
        cost_estimate=pl.CostEstimate(
            flops=8 * rows * tokens, bytes_accessed=32 * rows * tokens, transcendentals=0
        ),
        compiler_params=pltpu.CompilerParams(vmem_limit_bytes=24 * 1024 * 1024),
        name=name,
    )(ids, clips, ring)


def product_kernel(s_ref, *refs):
    acts, out_ref = refs[:-1], refs[-1]
    tokens = s_ref.shape[2]
    total = None
    first = 0
    for a_ref in acts:
        count = a_ref.shape[0]
        m, start = first // tokens, first % tokens
        part = jnp.dot(s_ref[m, :, start : start + count], a_ref[...], preferred_element_type=F32)
        total = part if total is None else total + part
        first += count
    out_ref[...] = total.astype(out_ref.dtype)


def product(name, scaled, acts, width, tile, dtype):
    members, rows, tokens = scaled.shape
    depth = members * tokens

    def spec(height, first):
        return pl.BlockSpec((height, tile), lambda j: (0, j + first // tile))

    return pl.pallas_call(
        product_kernel,
        out_shape=jax.ShapeDtypeStruct((rows, width), dtype),
        grid=(width // tile,),
        in_specs=[pl.BlockSpec((members, rows, tokens), lambda j: (0, 0, 0))]
        + [spec(a.shape[0], first) for a, first in acts],
        out_specs=spec(rows, 0),
        cost_estimate=pl.CostEstimate(
            flops=2 * rows * depth * width,
            bytes_accessed=2 * (rows * depth + depth * width + rows * width),
            transcendentals=0,
        ),
        compiler_params=pltpu.CompilerParams(vmem_limit_bytes=40 * 1024 * 1024),
        name=name,
    )(scaled, *[a for a, _ in acts])


def shards(acts, out_grads, other_sq, noise):
    dp, te = lax.axis_index("dp"), lax.axis_index("tensor")
    y, xh, xl, z = dp // 4, (dp // 2) % 2, te // NZ, te % NZ
    examples, seq, columns = acts.shape
    tokens = examples * seq
    features = out_grads.shape[2]
    rows = features // 2
    tile = columns // 3
    stage = lax.optimization_barrier
    ids = dp.reshape(1).astype(jnp.int32)

    grads_t = out_grads.reshape(tokens, features).T
    routes = [spread(0), spread(1)]
    sources = [send(grads_t, inside) for inside, _ in routes]

    def blocks(x):
        gram = jnp.einsum("btf,bsf->bts", x, x, preferred_element_type=F32).astype(BF)
        mid = seq // 2
        return jnp.stack([gram[:, :mid, :mid], gram[:, :mid, mid:], gram[:, mid:, mid:]])

    grams = jnp.stack([blocks(acts), blocks(out_grads)])
    flat = acts.reshape(tokens, columns)
    grams, flat = stage((grams, flat))

    def near(part):
        return send(part, along_y(1)), send(part, along_y(-1))

    def halved(grams, bit, perm):
        low, high = jnp.split(grams, 2, axis=3)
        keep, give = jnp.where(bit == 0, low, high), jnp.where(bit == 0, high, low)
        return (keep.astype(F32) + send(give, perm).astype(F32)).astype(BF)

    below0, above0 = near(flat[:, :tile])
    sibling = send(flat, CORE)
    grams = halved(grams, xl, XLO)
    sources, grams, below0, above0 = stage((sources, grams, below0, above0))
    sources = [send(block, steps) for block, (_, steps) in zip(sources, routes)]
    grams = halved(grams, z % 2, flip_z(1))
    sources, grams, flat = stage((sources, grams, flat))
    below1, above1 = near(flat[:, tile:])

    turn = xl ^ (y // 2) ^ xh
    z_rings = [list(range(first, first + NZ)) for first in (0, NZ)]
    theirs, mine = [
        lax.all_gather(
            jnp.where(turn == t, sources[0], sources[1])[None],
            "tensor",
            axis=0,
            tiled=True,
            axis_index_groups=z_rings,
        )
        for t in (1, 0)
    ]
    for bit, perm in (((z // 2) % 2, flip_z(2)), (z // 4, flip_z(4))):
        grams = halved(grams, bit, perm)
    grams = grams.astype(F32)
    weight = jnp.array([1.0, 2.0, 1.0], F32)[:, None, None, None]
    total = jnp.sum(grams[0] * grams[1] * weight, axis=(0, 2, 3)) + jnp.sum(other_sq, axis=1)
    for perm in (XLO, flip_z(1), flip_z(2), flip_z(4)):
        total = total + send(total, perm)
    clip = jnp.minimum(1.0, clip_norm / jnp.sqrt(total))

    clip, below1, above1 = stage((clip, below1, above1))
    columns_y = [[4 * k + 2 * x + core for k in range(NY) for core in range(2)] for x in range(2)]
    clips = lax.all_to_all(
        jnp.broadcast_to(clip, (2 * NY, examples)),
        "dp",
        0,
        0,
        tiled=True,
        axis_index_groups=columns_y,
    ).reshape(-1)
    clips, below0, above0, below1, above1 = stage((clips, below0, above0, below1, above1))

    def ahead(first, second):
        return jnp.concatenate([first, second[:, :tile]], axis=1)

    far = [
        send(ahead(below0[:seq], below1[:seq]), along_y(1)),
        send(ahead(above0[seq:], above1[seq:]), along_y(-1)),
    ]
    far2 = [send(below1[:seq, tile:], along_y(1)), send(above1[seq:, tile:], along_y(-1))]

    def swap(array):
        return send(array, CORE)

    near0 = [above0, swap(above0)], [below0, swap(below0)]
    near1 = [above1, swap(above1)], [below1, swap(below1)]

    def held(k, near, first, far, first_far):
        parts = [(flat, k * tile), (sibling, k * tile)] + [(a, first) for a in near[0]]
        parts += [(a, first_far) for a in far + [swap(a) for a in far]]
        return parts + [(a, first) for a in near[1]]

    scaled = scale_grads("scale_theirs", ids, clips, theirs)
    early = [held(0, near0, 0, far, 0), held(1, near1, 0, far, tile)]
    part = product("theirs_0", scaled, early[0], tile, tile, BF)
    part, far2, scaled = stage((part, far2, scaled))
    part = jnp.concatenate([part, product("theirs_1", scaled, early[1], tile, tile, BF)], axis=1)
    low, high = send(part[:rows], along_x(1)), send(part[rows:], along_x(-1))
    low, high = stage((low, high))
    low, high = send(low, along_x(1)), send(high, along_x(-1))

    late = held(2, near1, tile, far2, 0)
    part = product("theirs_2", scaled, late, tile, tile, BF)
    part, mine = stage((part, mine))
    low2, high2 = send(part[:rows], along_x(1)), send(part[rows:], along_x(-1))
    scaled = scale_grads("scale_mine", ids, clips, mine)
    own = [product(f"mine_{k}", scaled, early[k], tile, tile, F32) for k in range(2)]
    low2, high2 = send(low2, along_x(1)), send(high2, along_x(-1))
    own.append(product("mine_2", scaled, late, tile, tile, F32))

    width = features * 2 * NZ
    factor = math.sqrt(columns * 2 * NZ * width) / clip_norm
    root = math.sqrt(examples * 4 * NY)
    parts = []
    for k in range(3):
        up, down = (low2, high2) if k == 2 else (low, high)
        first = 0 if k == 2 else k * tile
        got = jnp.concatenate([a[:, first : first + tile] for a in (up, down)]).astype(F32)
        parts.append((factor * (own[k] + got) + noise[:, k * tile : (k + 1) * tile]) / root)
    return jnp.concatenate(parts, axis=1)


def solution(mesh):
    placed = (
        P("dp", None, "tensor"),
        P("dp", None, "tensor"),
        P("dp", "tensor"),
        P("dp", "tensor"),
    )
    return jax.shard_map(
        shards, mesh=mesh, in_specs=placed, out_specs=P("dp", "tensor"), check_vma=False
    )
```

```python
import math

import jax
import jax.numpy as jnp
from jax import lax
from jax.experimental import pallas as pl
from jax.experimental.pallas import tpu as pltpu
from jax.sharding import PartitionSpec as P

clip_norm = 2.5
AXES = ("dp", "tensor")
NY, NX, NZ = 4, 4, 8
OFF = (0, 1, 2, -1)
BF = jnp.bfloat16
F32 = jnp.float32


def coords(i):
    dp, te = divmod(i, 2 * NZ)
    return dp // 4, (dp // 2) % 2, dp % 2, te // NZ, te % NZ


def index(y, xh, c, xl, z):
    return ((y % NY * 2 + xh) * 2 + c) * 2 * NZ + xl * NZ + z % NZ


def perm_of(move):
    return [(i, index(*move(*coords(i)))) for i in range(NY * NX * NZ * 2)]


def along_x(step):
    def move(y, xh, c, xl, z):
        x = (xh * 2 + xl + step) % NX
        return y, x // 2, c, x % 2, z

    return perm_of(move)


def along_y(step):
    return perm_of(lambda y, xh, c, xl, z: (y + step, xh, c, xl, z))


def along_z(step):
    return perm_of(lambda y, xh, c, xl, z: (y, xh, c, xl, z + step))


def flip_z(bit):
    return perm_of(lambda y, xh, c, xl, z: (y, xh, c, xl, z ^ bit))


def spread(flip):
    def move(y, xh, c, xl, z):
        t, u = (z // 2) % 2, z % 2
        m = 2 * (xh ^ t) + (c ^ u)
        return y, t, u, xl ^ flip, z + OFF[m]

    return perm_of(move)


CORE = perm_of(lambda y, xh, c, xl, z: (y, xh, 1 - c, xl, z))
XHI = perm_of(lambda y, xh, c, xl, z: (y, 1 - xh, c, xl, z))
XLO = perm_of(lambda y, xh, c, xl, z: (y, xh, c, 1 - xl, z))


def send(value, perm):
    return lax.ppermute(value, AXES, perm)


def scale_kernel(place_ref, clip_ref, *refs):
    pieces, out_ref = refs[:-1], refs[-1]
    dp, te = place_ref[0], place_ref[1]
    y, xh, c, xl, z = dp // 4, (dp // 2) % 2, dp % 2, te // NZ, te % NZ
    half = out_ref.shape[3] // 2
    for r in range(NZ):
        q = (z - r - 2 * xh - c + 2 * NZ) % NZ
        m = q % 4
        k = ((q + 1) // 4) % 2
        for f in range(2):
            step = (2 * ((f + xl) % 2) + k - y + 4) % 4
            slot = jnp.where(step == 0, 3, jnp.where(step == 1, 0, jnp.where(step == 2, 2, 1)))
            block = pieces[4 + f] if r == 4 else pieces[r + (r > 4)].at[f]
            member = (2 * (xh ^ (m // 2)) + (c ^ (m % 2)))
            for e in range(2):
                cols = slice(e * half, (e + 1) * half)
                out_ref[slot, m, :, cols] = (
                    clip_ref[2 * member + e] * block[:, cols].astype(F32)
                ).astype(BF)


def scale_grads(places, clips, pieces):
    _, rows, tokens = pieces[0].shape
    smem = pl.BlockSpec(memory_space=pltpu.SMEM)
    vmem = pl.BlockSpec(memory_space=pltpu.VMEM)
    return pl.pallas_call(
        scale_kernel,
        out_shape=jax.ShapeDtypeStruct((4, 4, rows, tokens), BF),
        in_specs=[smem, smem] + [vmem] * len(pieces),
        out_specs=vmem,
        cost_estimate=pl.CostEstimate(
            flops=16 * rows * tokens, bytes_accessed=rows * tokens, transcendentals=0
        ),
        compiler_params=pltpu.CompilerParams(vmem_limit_bytes=24 * 1024 * 1024),
        name="scale_grads",
    )(places, clips, *pieces)


def product_kernel(s_ref, *refs):
    acts, outs = refs[:6], refs[6:]
    slots, _, rows, tokens = s_ref.shape
    total = None
    first = 0
    for a_ref in acts:
        count = a_ref.shape[0]
        m, start = first // tokens, first % tokens
        left = s_ref[:, m, :, start : start + count].reshape(slots * rows, count)
        part = jnp.dot(left, a_ref[...], preferred_element_type=F32)
        total = part if total is None else total + part
        first += count
    first = 0
    for out_ref in outs:
        count = out_ref.shape[0]
        out_ref[...] = total[first : first + count].astype(out_ref.dtype)
        first += count


def product(name, scaled, first, slots, acts, tile, parts, dtype):
    _, quarters, rows, tokens = scaled.shape
    width = acts[0].shape[1]
    count = slots * rows // parts
    return pl.pallas_call(
        product_kernel,
        out_shape=[jax.ShapeDtypeStruct((count, width), dtype)] * parts,
        grid=(width // tile,),
        in_specs=[
            pl.BlockSpec((slots, quarters, rows, tokens), lambda j: (first // slots, 0, 0, 0))
        ]
        + [pl.BlockSpec((a.shape[0], tile), lambda j: (0, j)) for a in acts],
        out_specs=[pl.BlockSpec((count, tile), lambda j: (0, j))] * parts,
        cost_estimate=pl.CostEstimate(
            flops=2 * slots * rows * width, bytes_accessed=2 * rows * width, transcendentals=0
        ),
        compiler_params=pltpu.CompilerParams(vmem_limit_bytes=24 * 1024 * 1024),
        name=name,
    )(scaled, *acts)


def all_to_all(value, axis, groups):
    return lax.all_to_all(value, axis, 0, 0, tiled=True, axis_index_groups=groups)


def shards(acts, out_grads, other_sq, noise):
    dp, te = lax.axis_index("dp"), lax.axis_index("tensor")
    y, xh, c, xl, z = dp // 4, (dp // 2) % 2, dp % 2, te // NZ, te % NZ
    examples, seq, columns = acts.shape
    tokens = examples * seq
    features = out_grads.shape[2]
    rows = features // 2
    stage = lax.optimization_barrier
    z_rings = [list(range(first, first + NZ)) for first in (0, NZ)]
    chip_pairs = [list(range(first, first + 4)) for first in range(0, 4 * NY, 4)]

    flat = acts.reshape(tokens, columns)
    grads_t = out_grads.reshape(tokens, features).T
    sources = [send(grads_t, spread(0)), send(grads_t, spread(1))]

    def blocks(x):
        gram = jnp.einsum("btf,bsf->bts", x, x, preferred_element_type=F32).astype(BF)
        mid = seq // 2
        return jnp.stack([gram[:, :mid, :mid], gram[:, :mid, mid:], gram[:, mid:, mid:]])

    grams = jnp.stack([blocks(acts), blocks(out_grads)])
    low, high = jnp.split(grams, 2, axis=3)
    keep, give = jnp.where(xl == 0, low, high), jnp.where(xl == 0, high, low)
    grams = (keep.astype(F32) + send(give, XLO).astype(F32)).astype(BF)
    sources, grams, flat = stage((sources, grams, flat))

    up = send(flat[:seq], along_x(1))
    down = send(flat[seq:], along_x(-1))
    own = jnp.stack(sources)
    shape = grams.shape
    grams = jnp.moveaxis(grams.reshape(shape[:3] + (NZ, -1, shape[4])), 3, 0)
    grams = all_to_all(grams, "tensor", z_rings).astype(F32).sum(axis=0)
    weight = jnp.array([1.0, 2.0, 1.0], F32)[:, None, None, None]
    total = jnp.sum(grams[0] * grams[1] * weight, axis=(0, 2, 3)) + jnp.sum(other_sq, axis=1)
    total = all_to_all(jnp.broadcast_to(total, (NZ, examples)), "tensor", z_rings).sum(axis=0)
    own, total = stage((own, total))

    fwd, bwd = [own, send(own, along_z(1))], [own, send(own, along_z(-1))]
    up, down, total = stage((up, down, total))
    total = total + send(total, XLO)
    clip = jnp.minimum(1.0, clip_norm / jnp.sqrt(total))
    clips = all_to_all(jnp.broadcast_to(clip, (4, examples)), "dp", chip_pairs).reshape(-1)
    up, down, fwd[1], bwd[1], clips = stage((up, down, fwd[1], bwd[1], clips))

    up, down = send(up, along_x(1)), send(down, along_x(-1))
    sibling = send(flat, CORE)
    for _ in range(2):
        fwd.append(send(fwd[-1], along_z(1)))
        bwd.append(send(bwd[-1], along_z(-1)))
    up, down, fwd[3], bwd[3] = stage((up, down, fwd[3], bwd[3]))

    far = [send(fwd[3][0], along_z(1)), send(bwd[3][1], along_z(-1))]
    up_sibling, down_sibling = send(up, CORE), send(down, CORE)
    pieces = [own, fwd[1], fwd[2], fwd[3], far[0], far[1], bwd[3], bwd[2], bwd[1]]
    places = jnp.stack([dp, te]).astype(jnp.int32)
    scaled = scale_grads(places, clips, pieces)

    held = [flat, sibling, up, down, up_sibling, down_sibling]
    tile = columns // 3
    far_a, far_b = product("product_far", scaled, 2, 1, held, tile, 2, BF)
    from_down, from_up = send(far_a, along_y(1)), send(far_b, along_y(-1))
    next_a, next_b, prev_a, prev_b = product("product_near", scaled, 0, 2, held, tile, 4, BF)
    next_b, prev_a = send(next_b, along_y(1)), send(prev_a, along_y(-1))
    next_a = (next_a.astype(F32) + from_down.astype(F32)).astype(BF)
    prev_b = (prev_b.astype(F32) + from_up.astype(F32)).astype(BF)
    next_a, prev_b, scaled = stage((next_a, prev_b, scaled))
    next_a, prev_b = send(next_a, along_y(1)), send(prev_b, along_y(-1))
    (mine,) = product("product_own", scaled, 3, 1, held, tile, 1, F32)

    width = features * 2 * NZ
    factor = math.sqrt(columns * 2 * NZ * width) / clip_norm
    root = math.sqrt(examples * 4 * NY)
    summed = jnp.concatenate(
        [next_a.astype(F32) + prev_a.astype(F32), next_b.astype(F32) + prev_b.astype(F32)]
    )
    return (factor * (mine + summed) + noise) / root


def solution(mesh):
    placed = (
        P("dp", None, "tensor"),
        P("dp", None, "tensor"),
        P("dp", "tensor"),
        P("dp", "tensor"),
    )
    return jax.shard_map(
        shards, mesh=mesh, in_specs=placed, out_specs=P("dp", "tensor"), check_vma=False
    )
```

```python
import math

import jax
import jax.numpy as jnp
from jax import lax
from jax.experimental import pallas as pl
from jax.experimental.pallas import tpu as pltpu
from jax.sharding import PartitionSpec as P

clip_norm = 2.5
AXES = ("dp", "tensor")
NY, NX, NZ = 4, 4, 8
OFF = (0, 1, 2, -1)
BF = jnp.bfloat16
F32 = jnp.float32


def coords(i):
    dp, te = divmod(i, 2 * NZ)
    return dp // 4, (dp // 2) % 2, dp % 2, te // NZ, te % NZ


def index(y, xh, c, xl, z):
    return ((y % NY * 2 + xh) * 2 + c) * 2 * NZ + xl * NZ + z % NZ


def perm_of(move):
    return [(i, index(*move(*coords(i)))) for i in range(NY * NX * NZ * 2)]


def along_x(step):
    def move(y, xh, c, xl, z):
        x = (xh * 2 + xl + step) % NX
        return y, x // 2, c, x % 2, z

    return perm_of(move)


def along_y(step):
    return perm_of(lambda y, xh, c, xl, z: (y + step, xh, c, xl, z))


def along_z(step):
    return perm_of(lambda y, xh, c, xl, z: (y, xh, c, xl, z + step))


def flip_z(bit):
    return perm_of(lambda y, xh, c, xl, z: (y, xh, c, xl, z ^ bit))


def spread(flip):
    def move(y, xh, c, xl, z):
        t, u = (z // 2) % 2, z % 2
        m = 2 * (xh ^ t) + (c ^ u)
        return y, t, u, xl ^ flip, z + OFF[m]

    return perm_of(move)


CORE = perm_of(lambda y, xh, c, xl, z: (y, xh, 1 - c, xl, z))
XHI = perm_of(lambda y, xh, c, xl, z: (y, 1 - xh, c, xl, z))
XLO = perm_of(lambda y, xh, c, xl, z: (y, xh, c, 1 - xl, z))


def send(value, perm):
    return lax.ppermute(value, AXES, perm)


def scale_kernel(place_ref, clip_ref, *refs):
    pieces, out_ref, held_ref, arrived = refs[:-3], refs[-3], refs[-2], refs[-1]
    dp, te = place_ref[0], place_ref[1]
    y, xh, c, xl, z = dp // 4, (dp // 2) % 2, dp % 2, te // NZ, te % NZ
    half = out_ref.shape[3] // 2
    copies = []
    for i, piece in enumerate(pieces):
        if i in (4, 5):
            place = held_ref.at[4 + i]
        else:
            place = held_ref.at[pl.ds(2 * (i - (i > 5)), 2)]
        copies.append(pltpu.make_async_copy(piece, place, arrived.at[i]))
    for copy in copies:
        copy.start()
    for r in range(NZ):
        q = (z - r - 2 * xh - c + 2 * NZ) % NZ
        m = q % 4
        k = ((q + 1) // 4) % 2
        member = 2 * (xh ^ (m // 2)) + (c ^ (m % 2))
        for copy in copies[4:6] if r == 4 else [copies[r + (r > 4)]]:
            copy.wait()
        for f in range(2):
            step = (2 * ((f + xl) % 2) + k - y + 4) % 4
            slot = jnp.where(step == 0, 3, jnp.where(step == 1, 0, jnp.where(step == 2, 2, 1)))
            for e in range(2):
                cols = slice(e * half, (e + 1) * half)
                out_ref[slot, m, :, cols] = (
                    clip_ref[2 * member + e] * held_ref[2 * r + f, :, cols].astype(F32)
                ).astype(BF)


def scale_grads(places, clips, pieces):
    _, rows, tokens = pieces[0].shape
    smem = pl.BlockSpec(memory_space=pltpu.SMEM)
    return pl.pallas_call(
        scale_kernel,
        out_shape=jax.ShapeDtypeStruct((4, 4, rows, tokens), BF),
        in_specs=[smem, smem] + [pl.BlockSpec(memory_space=pl.ANY)] * len(pieces),
        out_specs=pl.BlockSpec(memory_space=pltpu.VMEM),
        scratch_shapes=[
            pltpu.VMEM((2 * NZ, rows, tokens), BF),
            pltpu.SemaphoreType.DMA((len(pieces),)),
        ],
        cost_estimate=pl.CostEstimate(
            flops=16 * rows * tokens, bytes_accessed=rows * tokens, transcendentals=0
        ),
        compiler_params=pltpu.CompilerParams(vmem_limit_bytes=24 * 1024 * 1024),
        name="scale_grads",
    )(places, clips, *pieces)


def product_kernel(s_ref, *refs):
    acts, outs = refs[:6], refs[6:]
    slots, _, rows, tokens = s_ref.shape
    total = None
    first = 0
    for a_ref in acts:
        count = a_ref.shape[0]
        m, start = first // tokens, first % tokens
        left = s_ref[:, m, :, start : start + count].reshape(slots * rows, count)
        part = jnp.dot(left, a_ref[...], preferred_element_type=F32)
        total = part if total is None else total + part
        first += count
    first = 0
    for out_ref in outs:
        count = out_ref.shape[0]
        out_ref[...] = total[first : first + count].astype(out_ref.dtype)
        first += count


def product(name, scaled, first, slots, acts, tile, parts, dtype):
    _, quarters, rows, tokens = scaled.shape
    width = acts[0].shape[1]
    count = slots * rows // parts
    return pl.pallas_call(
        product_kernel,
        out_shape=[jax.ShapeDtypeStruct((count, width), dtype)] * parts,
        grid=(width // tile,),
        in_specs=[
            pl.BlockSpec((slots, quarters, rows, tokens), lambda j: (first // slots, 0, 0, 0))
        ]
        + [pl.BlockSpec((a.shape[0], tile), lambda j: (0, j)) for a in acts],
        out_specs=[pl.BlockSpec((count, tile), lambda j: (0, j))] * parts,
        cost_estimate=pl.CostEstimate(
            flops=2 * slots * rows * width, bytes_accessed=2 * rows * width, transcendentals=0
        ),
        compiler_params=pltpu.CompilerParams(vmem_limit_bytes=24 * 1024 * 1024),
        name=name,
    )(scaled, *acts)


def all_to_all(value, axis, groups):
    return lax.all_to_all(value, axis, 0, 0, tiled=True, axis_index_groups=groups)


def shards(acts, out_grads, other_sq, noise):
    dp, te = lax.axis_index("dp"), lax.axis_index("tensor")
    y, xh, c, xl, z = dp // 4, (dp // 2) % 2, dp % 2, te // NZ, te % NZ
    examples, seq, columns = acts.shape
    tokens = examples * seq
    features = out_grads.shape[2]
    rows = features // 2
    stage = lax.optimization_barrier
    z_rings = [list(range(first, first + NZ)) for first in (0, NZ)]
    chip_pairs = [list(range(first, first + 4)) for first in range(0, 4 * NY, 4)]

    flat = acts.reshape(tokens, columns)
    grads_t = out_grads.reshape(tokens, features).T
    sources = [send(grads_t, spread(0)), send(grads_t, spread(1))]

    def blocks(x):
        gram = jnp.einsum("btf,bsf->bts", x, x, preferred_element_type=F32).astype(BF)
        mid = seq // 2
        return jnp.stack([gram[:, :mid, :mid], gram[:, :mid, mid:], gram[:, mid:, mid:]])

    grams = jnp.stack([blocks(acts), blocks(out_grads)])
    grams = (grams.astype(F32) + send(grams, XLO).astype(F32)).astype(BF)
    others = jnp.sum(other_sq, axis=1)
    others = others + send(others, XLO)
    sources, grams, flat, others = stage((sources, grams, flat, others))

    up = send(flat[:seq], along_x(1))
    down = send(flat[seq:], along_x(-1))
    own = jnp.stack(sources)
    fwd, bwd = [own, send(own, along_z(1))], [own, send(own, along_z(-1))]
    shape = grams.shape
    grams = jnp.moveaxis(grams.reshape(shape[:3] + (NZ, -1, shape[4])), 3, 0)
    grams = all_to_all(grams, "tensor", z_rings).astype(F32).sum(axis=0)
    weight = jnp.array([1.0, 2.0, 1.0], F32)[:, None, None, None]
    total = jnp.sum(grams[0] * grams[1] * weight, axis=(0, 2, 3)) + others
    up, down, fwd[1], bwd[1], total = stage((up, down, fwd[1], bwd[1], total))

    up, down = send(up, along_x(1)), send(down, along_x(-1))
    fwd.append(send(fwd[1], along_z(1)))
    bwd.append(send(bwd[1], along_z(-1)))
    sibling = send(flat, CORE)
    total = all_to_all(jnp.broadcast_to(total, (NZ, examples)), "tensor", z_rings).sum(axis=0)
    fwd[2], bwd[2], total = stage((fwd[2], bwd[2], total))

    fwd.append(send(fwd[2], along_z(1)))
    bwd.append(send(bwd[2], along_z(-1)))
    clip = jnp.minimum(1.0, clip_norm / jnp.sqrt(total))
    clips = all_to_all(jnp.broadcast_to(clip, (4, examples)), "dp", chip_pairs).reshape(-1)
    fwd[3], bwd[3], clips, up, down = stage((fwd[3], bwd[3], clips, up, down))

    far = [send(fwd[3][0], along_z(1)), send(bwd[3][1], along_z(-1))]
    up_sibling, down_sibling = send(up, CORE), send(down, CORE)
    pieces = [own, fwd[1], fwd[2], fwd[3], far[0], far[1], bwd[3], bwd[2], bwd[1]]
    places = jnp.stack([dp, te]).astype(jnp.int32)
    scaled = scale_grads(places, clips, pieces)

    held = [flat, sibling, up, down, up_sibling, down_sibling]
    tile = columns // 3
    far_a, far_b = product("product_far", scaled, 2, 1, held, tile, 2, BF)
    from_down, from_up = send(far_a, along_y(1)), send(far_b, along_y(-1))
    next_a, next_b, prev_a, prev_b = product("product_near", scaled, 0, 2, held, tile, 4, BF)
    next_b, prev_a = send(next_b, along_y(1)), send(prev_a, along_y(-1))
    next_a = (next_a.astype(F32) + from_down.astype(F32)).astype(BF)
    prev_b = (prev_b.astype(F32) + from_up.astype(F32)).astype(BF)
    next_a, prev_b, scaled = stage((next_a, prev_b, scaled))
    next_a, prev_b = send(next_a, along_y(1)), send(prev_b, along_y(-1))
    (mine,) = product("product_own", scaled, 3, 1, held, tile, 1, F32)

    width = features * 2 * NZ
    factor = math.sqrt(columns * 2 * NZ * width) / clip_norm
    root = math.sqrt(examples * 4 * NY)
    summed = jnp.concatenate(
        [next_a.astype(F32) + prev_a.astype(F32), next_b.astype(F32) + prev_b.astype(F32)]
    )
    return (factor * (mine + summed) + noise) / root


def solution(mesh):
    placed = (
        P("dp", None, "tensor"),
        P("dp", None, "tensor"),
        P("dp", "tensor"),
        P("dp", "tensor"),
    )
    return jax.shard_map(
        shards, mesh=mesh, in_specs=placed, out_specs=P("dp", "tensor"), check_vma=False
    )
```

```python
import math

import jax
import jax.numpy as jnp
from jax import lax
from jax.experimental import pallas as pl
from jax.experimental.pallas import tpu as pltpu
from jax.sharding import PartitionSpec as P

clip_norm = 2.5
AXES = ("dp", "tensor")
NY, NX, NZ = 4, 4, 8
OFF = (0, 1, 2, -1)
BF = jnp.bfloat16
F32 = jnp.float32


def coords(i):
    dp, te = divmod(i, 2 * NZ)
    return dp // 4, (dp // 2) % 2, dp % 2, te // NZ, te % NZ


def index(y, xh, c, xl, z):
    return ((y % NY * 2 + xh) * 2 + c) * 2 * NZ + xl * NZ + z % NZ


def perm_of(move):
    return [(i, index(*move(*coords(i)))) for i in range(NY * NX * NZ * 2)]


def along_x(step):
    def move(y, xh, c, xl, z):
        x = (xh * 2 + xl + step) % NX
        return y, x // 2, c, x % 2, z

    return perm_of(move)


def along_y(step):
    return perm_of(lambda y, xh, c, xl, z: (y + step, xh, c, xl, z))


def along_z(step):
    return perm_of(lambda y, xh, c, xl, z: (y, xh, c, xl, z + step))


def flip_z(bit):
    return perm_of(lambda y, xh, c, xl, z: (y, xh, c, xl, z ^ bit))


def spread(flip):
    def move(y, xh, c, xl, z):
        t, u = (z // 2) % 2, z % 2
        m = 2 * (xh ^ t) + (c ^ u)
        return y, t, u, xl ^ flip, z + OFF[m]

    return perm_of(move)


CORE = perm_of(lambda y, xh, c, xl, z: (y, xh, 1 - c, xl, z))
XHI = perm_of(lambda y, xh, c, xl, z: (y, 1 - xh, c, xl, z))
XLO = perm_of(lambda y, xh, c, xl, z: (y, xh, c, 1 - xl, z))


def send(value, perm):
    return lax.ppermute(value, AXES, perm)


def scale_kernel(place_ref, clip_ref, *refs):
    pieces, out_ref, held_ref, arrived = refs[:-3], refs[-3], refs[-2], refs[-1]
    dp, te = place_ref[0], place_ref[1]
    y, xh, c, xl, z = dp // 4, (dp // 2) % 2, dp % 2, te // NZ, te % NZ
    half = out_ref.shape[3] // 2
    copies = []
    for i, piece in enumerate(pieces):
        if i in (4, 5):
            place = held_ref.at[4 + i]
        else:
            place = held_ref.at[pl.ds(2 * (i - (i > 5)), 2)]
        copies.append(pltpu.make_async_copy(piece, place, arrived.at[i]))
    for copy in copies:
        copy.start()
    for r in range(NZ):
        q = (z - r - 2 * xh - c + 2 * NZ) % NZ
        m = q % 4
        k = ((q + 1) // 4) % 2
        member = 2 * (xh ^ (m // 2)) + (c ^ (m % 2))
        for copy in copies[4:6] if r == 4 else [copies[r + (r > 4)]]:
            copy.wait()
        for f in range(2):
            step = (2 * ((f + xl) % 2) + k - y + 4) % 4
            slot = jnp.where(step == 0, 3, jnp.where(step == 1, 0, jnp.where(step == 2, 2, 1)))
            for e in range(2):
                cols = slice(e * half, (e + 1) * half)
                out_ref[slot, m, :, cols] = (
                    clip_ref[2 * member + e] * held_ref[2 * r + f, :, cols].astype(F32)
                ).astype(BF)


def scale_grads(places, clips, pieces):
    _, rows, tokens = pieces[0].shape
    smem = pl.BlockSpec(memory_space=pltpu.SMEM)
    return pl.pallas_call(
        scale_kernel,
        out_shape=jax.ShapeDtypeStruct((4, 4, rows, tokens), BF),
        in_specs=[smem, smem] + [pl.BlockSpec(memory_space=pl.ANY)] * len(pieces),
        out_specs=pl.BlockSpec(memory_space=pltpu.VMEM),
        scratch_shapes=[
            pltpu.VMEM((2 * NZ, rows, tokens), BF),
            pltpu.SemaphoreType.DMA((len(pieces),)),
        ],
        cost_estimate=pl.CostEstimate(
            flops=16 * rows * tokens, bytes_accessed=rows * tokens, transcendentals=0
        ),
        compiler_params=pltpu.CompilerParams(vmem_limit_bytes=24 * 1024 * 1024),
        name="scale_grads",
    )(places, clips, *pieces)


def product_kernel(s_ref, *refs):
    acts, outs = refs[:6], refs[6:]
    slots, _, rows, tokens = s_ref.shape
    total = None
    first = 0
    for a_ref in acts:
        count = a_ref.shape[0]
        m, start = first // tokens, first % tokens
        left = s_ref[:, m, :, start : start + count].reshape(slots * rows, count)
        part = jnp.dot(left, a_ref[...], preferred_element_type=F32)
        total = part if total is None else total + part
        first += count
    first = 0
    for out_ref in outs:
        count = out_ref.shape[0]
        out_ref[...] = total[first : first + count].astype(out_ref.dtype)
        first += count


def product(name, scaled, first, slots, acts, tile, parts, dtype):
    _, quarters, rows, tokens = scaled.shape
    width = acts[0].shape[1]
    count = slots * rows // parts
    return pl.pallas_call(
        product_kernel,
        out_shape=[jax.ShapeDtypeStruct((count, width), dtype)] * parts,
        grid=(width // tile,),
        in_specs=[
            pl.BlockSpec((slots, quarters, rows, tokens), lambda j: (first // slots, 0, 0, 0))
        ]
        + [pl.BlockSpec((a.shape[0], tile), lambda j: (0, j)) for a in acts],
        out_specs=[pl.BlockSpec((count, tile), lambda j: (0, j))] * parts,
        cost_estimate=pl.CostEstimate(
            flops=2 * slots * rows * width, bytes_accessed=2 * rows * width, transcendentals=0
        ),
        compiler_params=pltpu.CompilerParams(vmem_limit_bytes=24 * 1024 * 1024),
        name=name,
    )(scaled, *acts)


def all_to_all(value, axis, groups):
    return lax.all_to_all(value, axis, 0, 0, tiled=True, axis_index_groups=groups)


def shards(acts, out_grads, other_sq, noise):
    dp, te = lax.axis_index("dp"), lax.axis_index("tensor")
    y, xh, c, xl, z = dp // 4, (dp // 2) % 2, dp % 2, te // NZ, te % NZ
    examples, seq, columns = acts.shape
    tokens = examples * seq
    features = out_grads.shape[2]
    rows = features // 2
    stage = lax.optimization_barrier
    z_rings = [list(range(first, first + NZ)) for first in (0, NZ)]
    chip_pairs = [list(range(first, first + 4)) for first in range(0, 4 * NY, 4)]

    flat = acts.reshape(tokens, columns)
    grads_t = out_grads.reshape(tokens, features).T
    sources = [send(grads_t, spread(0)), send(grads_t, spread(1))]

    def blocks(x):
        gram = jnp.einsum("btf,bsf->bts", x, x, preferred_element_type=F32).astype(BF)
        mid = seq // 2
        return jnp.stack([gram[:, :mid, :mid], gram[:, :mid, mid:], gram[:, mid:, mid:]])

    grams = jnp.stack([blocks(acts), blocks(out_grads)])
    grams = (grams.astype(F32) + send(grams, XLO).astype(F32)).astype(BF)
    others = jnp.sum(other_sq, axis=1)
    others = others + send(others, XLO)
    sources, grams, flat, others = stage((sources, grams, flat, others))

    up = send(flat[:seq], along_x(1))
    down = send(flat[seq:], along_x(-1))
    own = jnp.stack(sources)
    fwd, bwd = [own], [own]

    def step_z():
        fwd.append(send(fwd[-1], along_z(1)))
        bwd.append(send(bwd[-1], along_z(-1)))

    step_z()
    fwd[1], bwd[1], grams = stage((fwd[1], bwd[1], grams))

    step_z()
    shape = grams.shape
    grams = jnp.moveaxis(grams.reshape(shape[:3] + (NZ, -1, shape[4])), 3, 0)
    grams = all_to_all(grams, "tensor", z_rings).astype(F32).sum(axis=0)
    weight = jnp.array([1.0, 2.0, 1.0], F32)[:, None, None, None]
    total = jnp.sum(grams[0] * grams[1] * weight, axis=(0, 2, 3)) + others
    up, down, fwd[2], bwd[2], total = stage((up, down, fwd[2], bwd[2], total))

    step_z()
    up, down = send(up, along_x(1)), send(down, along_x(-1))
    sibling = send(flat, CORE)
    total = all_to_all(jnp.broadcast_to(total, (NZ, examples)), "tensor", z_rings).sum(axis=0)
    fwd[3], bwd[3], total = stage((fwd[3], bwd[3], total))

    far = [send(fwd[3][0], along_z(1)), send(bwd[3][1], along_z(-1))]
    clip = jnp.minimum(1.0, clip_norm / jnp.sqrt(total))
    clips = all_to_all(jnp.broadcast_to(clip, (4, examples)), "dp", chip_pairs).reshape(-1)
    far[0], far[1], clips, up, down = stage((far[0], far[1], clips, up, down))
    up_sibling, down_sibling = send(up, CORE), send(down, CORE)
    pieces = [own, fwd[1], fwd[2], fwd[3], far[0], far[1], bwd[3], bwd[2], bwd[1]]
    places = jnp.stack([dp, te]).astype(jnp.int32)
    scaled = scale_grads(places, clips, pieces)

    held = [flat, sibling, up, down, up_sibling, down_sibling]
    tile = columns // 3
    far_a, far_b = product("product_far", scaled, 2, 1, held, tile, 2, BF)
    from_down, from_up = send(far_a, along_y(1)), send(far_b, along_y(-1))
    next_a, next_b, prev_a, prev_b = product("product_near", scaled, 0, 2, held, tile, 4, BF)
    next_b, prev_a = send(next_b, along_y(1)), send(prev_a, along_y(-1))
    next_a = (next_a.astype(F32) + from_down.astype(F32)).astype(BF)
    prev_b = (prev_b.astype(F32) + from_up.astype(F32)).astype(BF)
    next_a, prev_b, scaled = stage((next_a, prev_b, scaled))
    next_a, prev_b = send(next_a, along_y(1)), send(prev_b, along_y(-1))
    next_b, prev_a, scaled = stage((next_b, prev_a, scaled))
    (mine,) = product("product_own", scaled, 3, 1, held, tile, 1, F32)

    width = features * 2 * NZ
    factor = math.sqrt(columns * 2 * NZ * width) / clip_norm
    root = math.sqrt(examples * 4 * NY)
    summed = jnp.concatenate(
        [next_a.astype(F32) + prev_a.astype(F32), next_b.astype(F32) + prev_b.astype(F32)]
    )
    return (factor * (mine + summed) + noise) / root


def solution(mesh):
    placed = (
        P("dp", None, "tensor"),
        P("dp", None, "tensor"),
        P("dp", "tensor"),
        P("dp", "tensor"),
    )
    return jax.shard_map(
        shards, mesh=mesh, in_specs=placed, out_specs=P("dp", "tensor"), check_vma=False
    )
```

```python
import math

import jax
import jax.numpy as jnp
from jax import lax
from jax.experimental import pallas as pl
from jax.experimental.pallas import tpu as pltpu
from jax.sharding import PartitionSpec as P

clip_norm = 2.5
AXES = ("dp", "tensor")
NY, NX, NZ = 4, 4, 8
OFF = (0, 1, 2, -1)
BF = jnp.bfloat16
F32 = jnp.float32


def coords(i):
    dp, te = divmod(i, 2 * NZ)
    return dp // 4, (dp // 2) % 2, dp % 2, te // NZ, te % NZ


def index(y, xh, c, xl, z):
    return ((y % NY * 2 + xh) * 2 + c) * 2 * NZ + xl * NZ + z % NZ


def perm_of(move):
    return [(i, index(*move(*coords(i)))) for i in range(NY * NX * NZ * 2)]


def along_x(step):
    def move(y, xh, c, xl, z):
        x = (xh * 2 + xl + step) % NX
        return y, x // 2, c, x % 2, z

    return perm_of(move)


def along_y(step):
    return perm_of(lambda y, xh, c, xl, z: (y + step, xh, c, xl, z))


def along_z(step):
    return perm_of(lambda y, xh, c, xl, z: (y, xh, c, xl, z + step))


def flip_z(bit):
    return perm_of(lambda y, xh, c, xl, z: (y, xh, c, xl, z ^ bit))


def spread(flip):
    def move(y, xh, c, xl, z):
        t, u = (z // 2) % 2, z % 2
        m = 2 * (xh ^ t) + (c ^ u)
        return y, t, u, xl ^ flip, z + OFF[m]

    return perm_of(move)


CORE = perm_of(lambda y, xh, c, xl, z: (y, xh, 1 - c, xl, z))
XHI = perm_of(lambda y, xh, c, xl, z: (y, 1 - xh, c, xl, z))
XLO = perm_of(lambda y, xh, c, xl, z: (y, xh, c, 1 - xl, z))


def send(value, perm):
    return lax.ppermute(value, AXES, perm)


def scale_kernel(place_ref, clip_ref, *refs):
    pieces, out_ref, held_ref, arrived = refs[:-3], refs[-3], refs[-2], refs[-1]
    dp, te = place_ref[0], place_ref[1]
    y, xh, c, xl, z = dp // 4, (dp // 2) % 2, dp % 2, te // NZ, te % NZ
    half = out_ref.shape[3] // 2
    copies = []
    for i, piece in enumerate(pieces):
        if i in (4, 5):
            place = held_ref.at[4 + i]
        else:
            place = held_ref.at[pl.ds(2 * (i - (i > 5)), 2)]
        copies.append(pltpu.make_async_copy(piece, place, arrived.at[i]))
    for copy in copies:
        copy.start()
    for r in range(NZ):
        q = (z - r - 2 * xh - c + 2 * NZ) % NZ
        m = q % 4
        k = ((q + 1) // 4) % 2
        member = 2 * (xh ^ (m // 2)) + (c ^ (m % 2))
        for copy in copies[4:6] if r == 4 else [copies[r + (r > 4)]]:
            copy.wait()
        for f in range(2):
            step = (2 * ((f + xl) % 2) + k - y + 4) % 4
            slot = jnp.where(step == 0, 3, jnp.where(step == 1, 0, jnp.where(step == 2, 2, 1)))
            for e in range(2):
                cols = slice(e * half, (e + 1) * half)
                out_ref[slot, m, :, cols] = (
                    clip_ref[2 * member + e] * held_ref[2 * r + f, :, cols].astype(F32)
                ).astype(BF)


def scale_grads(places, clips, pieces):
    _, rows, tokens = pieces[0].shape
    smem = pl.BlockSpec(memory_space=pltpu.SMEM)
    return pl.pallas_call(
        scale_kernel,
        out_shape=jax.ShapeDtypeStruct((4, 4, rows, tokens), BF),
        in_specs=[smem, smem] + [pl.BlockSpec(memory_space=pl.ANY)] * len(pieces),
        out_specs=pl.BlockSpec(memory_space=pltpu.VMEM),
        scratch_shapes=[
            pltpu.VMEM((2 * NZ, rows, tokens), BF),
            pltpu.SemaphoreType.DMA((len(pieces),)),
        ],
        cost_estimate=pl.CostEstimate(
            flops=16 * rows * tokens, bytes_accessed=rows * tokens, transcendentals=0
        ),
        compiler_params=pltpu.CompilerParams(vmem_limit_bytes=24 * 1024 * 1024),
        name="scale_grads",
    )(places, clips, *pieces)


def product_kernel(s_ref, *refs):
    acts, outs = refs[:6], refs[6:]
    slots, _, rows, tokens = s_ref.shape
    total = None
    first = 0
    for a_ref in acts:
        count = a_ref.shape[0]
        m, start = first // tokens, first % tokens
        left = s_ref[:, m, :, start : start + count].reshape(slots * rows, count)
        part = jnp.dot(left, a_ref[...], preferred_element_type=F32)
        total = part if total is None else total + part
        first += count
    first = 0
    for out_ref in outs:
        count = out_ref.shape[0]
        out_ref[...] = total[first : first + count].astype(out_ref.dtype)
        first += count


def product(name, scaled, first, slots, acts, tile, parts, dtype):
    _, quarters, rows, tokens = scaled.shape
    width = acts[0].shape[1]
    count = slots * rows // parts
    return pl.pallas_call(
        product_kernel,
        out_shape=[jax.ShapeDtypeStruct((count, width), dtype)] * parts,
        grid=(width // tile,),
        in_specs=[
            pl.BlockSpec((slots, quarters, rows, tokens), lambda j: (first // slots, 0, 0, 0))
        ]
        + [pl.BlockSpec((a.shape[0], tile), lambda j: (0, j)) for a in acts],
        out_specs=[pl.BlockSpec((count, tile), lambda j: (0, j))] * parts,
        cost_estimate=pl.CostEstimate(
            flops=2 * slots * rows * width, bytes_accessed=2 * rows * width, transcendentals=0
        ),
        compiler_params=pltpu.CompilerParams(vmem_limit_bytes=24 * 1024 * 1024),
        name=name,
    )(scaled, *acts)


def all_to_all(value, axis, groups):
    return lax.all_to_all(value, axis, 0, 0, tiled=True, axis_index_groups=groups)


def shards(acts, out_grads, other_sq, noise):
    dp, te = lax.axis_index("dp"), lax.axis_index("tensor")
    y, xh, c, xl, z = dp // 4, (dp // 2) % 2, dp % 2, te // NZ, te % NZ
    examples, seq, columns = acts.shape
    tokens = examples * seq
    features = out_grads.shape[2]
    rows = features // 2
    stage = lax.optimization_barrier
    z_rings = [list(range(first, first + NZ)) for first in (0, NZ)]
    chip_pairs = [list(range(first, first + 4)) for first in range(0, 4 * NY, 4)]

    flat = acts.reshape(tokens, columns)
    grads_t = out_grads.reshape(tokens, features).T
    sources = [send(grads_t, spread(0)), send(grads_t, spread(1))]

    def blocks(x):
        gram = jnp.einsum("btf,bsf->bts", x, x, preferred_element_type=F32).astype(BF)
        mid = seq // 2
        return jnp.stack([gram[:, :mid, :mid], gram[:, :mid, mid:], gram[:, mid:, mid:]])

    grams = jnp.stack([blocks(acts), blocks(out_grads)])
    grams = (grams.astype(F32) + send(grams, XLO).astype(F32)).astype(BF)
    others = jnp.sum(other_sq, axis=1)
    others = others + send(others, XLO)
    own, grams, flat, others = stage((jnp.stack(sources), grams, flat, others))

    up = send(flat[:seq], along_x(1))
    down = send(flat[seq:], along_x(-1))
    sibling = send(flat, CORE)
    fwd, bwd = [own, send(own, along_z(1))], [own, send(own, along_z(-1))]
    shape = grams.shape
    grams = jnp.moveaxis(grams.reshape(shape[:3] + (NZ, -1, shape[4])), 3, 0)
    grams = all_to_all(grams, "tensor", z_rings).astype(F32).sum(axis=0)
    weight = jnp.array([1.0, 2.0, 1.0], F32)[:, None, None, None]
    total = jnp.sum(grams[0] * grams[1] * weight, axis=(0, 2, 3)) + others
    up, down, sibling, fwd[1], bwd[1], total = stage((up, down, sibling, fwd[1], bwd[1], total))

    up, down = send(up, along_x(1)), send(down, along_x(-1))
    fwd.append(send(fwd[1], along_z(1)))
    bwd.append(send(bwd[1], along_z(-1)))
    total = all_to_all(jnp.broadcast_to(total, (NZ, examples)), "tensor", z_rings).sum(axis=0)
    fwd[2], bwd[2], total = stage((fwd[2], bwd[2], total))

    fwd.append(send(fwd[2], along_z(1)))
    bwd.append(send(bwd[2], along_z(-1)))
    far = [send(fwd[2][0], along_z(2)), send(bwd[2][1], along_z(-2))]
    clip = jnp.minimum(1.0, clip_norm / jnp.sqrt(total))
    clips = all_to_all(jnp.broadcast_to(clip, (4, examples)), "dp", chip_pairs).reshape(-1)
    fwd[3], bwd[3], far, clips, up, down = stage((fwd[3], bwd[3], far, clips, up, down))
    up_sibling, down_sibling = send(up, CORE), send(down, CORE)
    pieces = [own, fwd[1], fwd[2], fwd[3], far[0], far[1], bwd[3], bwd[2], bwd[1]]
    places = jnp.stack([dp, te]).astype(jnp.int32)
    scaled = scale_grads(places, clips, pieces)

    held = [flat, sibling, up, down, up_sibling, down_sibling]
    tile = columns // 3
    far_a, far_b = product("product_far", scaled, 2, 1, held, tile, 2, BF)
    from_down, from_up = send(far_a, along_y(1)), send(far_b, along_y(-1))
    next_a, next_b, prev_a, prev_b = product("product_near", scaled, 0, 2, held, tile, 4, BF)
    next_b, prev_a = send(next_b, along_y(1)), send(prev_a, along_y(-1))
    next_a = (next_a.astype(F32) + from_down.astype(F32)).astype(BF)
    prev_b = (prev_b.astype(F32) + from_up.astype(F32)).astype(BF)
    next_a, prev_b, scaled = stage((next_a, prev_b, scaled))
    next_a, prev_b = send(next_a, along_y(1)), send(prev_b, along_y(-1))
    (mine,) = product("product_own", scaled, 3, 1, held, tile, 1, F32)

    width = features * 2 * NZ
    factor = math.sqrt(columns * 2 * NZ * width) / clip_norm
    root = math.sqrt(examples * 4 * NY)
    summed = jnp.concatenate(
        [next_a.astype(F32) + prev_a.astype(F32), next_b.astype(F32) + prev_b.astype(F32)]
    )
    return (factor * (mine + summed) + noise) / root


def solution(mesh):
    placed = (
        P("dp", None, "tensor"),
        P("dp", None, "tensor"),
        P("dp", "tensor"),
        P("dp", "tensor"),
    )
    return jax.shard_map(
        shards, mesh=mesh, in_specs=placed, out_specs=P("dp", "tensor"), check_vma=False
    )
```

```python
import math

import jax
import jax.numpy as jnp
from jax import lax
from jax.experimental import pallas as pl
from jax.experimental.pallas import tpu as pltpu
from jax.sharding import PartitionSpec as P

clip_norm = 2.5
AXES = ("dp", "tensor")
NY, NX, NZ = 4, 4, 8
OFF = (0, 1, 2, -1)
BF = jnp.bfloat16
F32 = jnp.float32


def coords(i):
    dp, te = divmod(i, 2 * NZ)
    return dp // 4, (dp // 2) % 2, dp % 2, te // NZ, te % NZ


def index(y, xh, c, xl, z):
    return ((y % NY * 2 + xh) * 2 + c) * 2 * NZ + xl * NZ + z % NZ


def perm_of(move):
    return [(i, index(*move(*coords(i)))) for i in range(NY * NX * NZ * 2)]


def along_x(step):
    def move(y, xh, c, xl, z):
        x = (xh * 2 + xl + step) % NX
        return y, x // 2, c, x % 2, z

    return perm_of(move)


def along_y(step):
    return perm_of(lambda y, xh, c, xl, z: (y + step, xh, c, xl, z))


def along_z(step):
    return perm_of(lambda y, xh, c, xl, z: (y, xh, c, xl, z + step))


def flip_z(bit):
    return perm_of(lambda y, xh, c, xl, z: (y, xh, c, xl, z ^ bit))


def spread(flip):
    def move(y, xh, c, xl, z):
        t, u = (z // 2) % 2, z % 2
        m = 2 * (xh ^ t) + (c ^ u)
        return y, t, u, xl ^ flip, z + OFF[m]

    return perm_of(move)


CORE = perm_of(lambda y, xh, c, xl, z: (y, xh, 1 - c, xl, z))
XHI = perm_of(lambda y, xh, c, xl, z: (y, 1 - xh, c, xl, z))
XLO = perm_of(lambda y, xh, c, xl, z: (y, xh, c, 1 - xl, z))


def send(value, perm):
    return lax.ppermute(value, AXES, perm)


def scale_kernel(place_ref, clip_ref, *refs):
    pieces, out_ref, held_ref, arrived = refs[:-3], refs[-3], refs[-2], refs[-1]
    dp, te = place_ref[0], place_ref[1]
    y, xh, c, xl, z = dp // 4, (dp // 2) % 2, dp % 2, te // NZ, te % NZ
    half = out_ref.shape[3] // 2
    copies = []
    for i, piece in enumerate(pieces):
        if i in (4, 5):
            place = held_ref.at[4 + i]
        else:
            place = held_ref.at[pl.ds(2 * (i - (i > 5)), 2)]
        copies.append(pltpu.make_async_copy(piece, place, arrived.at[i]))
    for copy in copies:
        copy.start()
    for r in range(NZ):
        q = (z - r - 2 * xh - c + 2 * NZ) % NZ
        m = q % 4
        k = ((q + 1) // 4) % 2
        member = 2 * (xh ^ (m // 2)) + (c ^ (m % 2))
        for copy in copies[4:6] if r == 4 else [copies[r + (r > 4)]]:
            copy.wait()
        for f in range(2):
            step = (2 * ((f + xl) % 2) + k - y + 4) % 4
            slot = jnp.where(step == 0, 3, jnp.where(step == 1, 0, jnp.where(step == 2, 2, 1)))
            for e in range(2):
                cols = slice(e * half, (e + 1) * half)
                out_ref[slot, m, :, cols] = (
                    clip_ref[2 * member + e] * held_ref[2 * r + f, :, cols].astype(F32)
                ).astype(BF)


def scale_grads(places, clips, pieces):
    _, rows, tokens = pieces[0].shape
    smem = pl.BlockSpec(memory_space=pltpu.SMEM)
    return pl.pallas_call(
        scale_kernel,
        out_shape=jax.ShapeDtypeStruct((4, 4, rows, tokens), BF),
        in_specs=[smem, smem] + [pl.BlockSpec(memory_space=pltpu.HBM)] * len(pieces),
        out_specs=pl.BlockSpec(memory_space=pltpu.VMEM),
        scratch_shapes=[
            pltpu.VMEM((2 * NZ, rows, tokens), BF),
            pltpu.SemaphoreType.DMA((len(pieces),)),
        ],
        cost_estimate=pl.CostEstimate(
            flops=16 * rows * tokens, bytes_accessed=rows * tokens, transcendentals=0
        ),
        compiler_params=pltpu.CompilerParams(vmem_limit_bytes=24 * 1024 * 1024),
        name="scale_grads",
    )(places, clips, *pieces)


def product_kernel(s_ref, *refs):
    acts, outs = refs[:6], refs[6:]
    slots, _, rows, tokens = s_ref.shape
    total = None
    first = 0
    for a_ref in acts:
        count = a_ref.shape[0]
        m, start = first // tokens, first % tokens
        left = s_ref[:, m, :, start : start + count].reshape(slots * rows, count)
        part = jnp.dot(left, a_ref[...], preferred_element_type=F32)
        total = part if total is None else total + part
        first += count
    first = 0
    for out_ref in outs:
        count = out_ref.shape[0]
        out_ref[...] = total[first : first + count].astype(out_ref.dtype)
        first += count


def product(name, scaled, first, slots, acts, tile, parts, dtype):
    _, quarters, rows, tokens = scaled.shape
    width = acts[0].shape[1]
    count = slots * rows // parts
    return pl.pallas_call(
        product_kernel,
        out_shape=[jax.ShapeDtypeStruct((count, width), dtype)] * parts,
        grid=(width // tile,),
        in_specs=[
            pl.BlockSpec((slots, quarters, rows, tokens), lambda j: (first // slots, 0, 0, 0))
        ]
        + [pl.BlockSpec((a.shape[0], tile), lambda j: (0, j)) for a in acts],
        out_specs=[pl.BlockSpec((count, tile), lambda j: (0, j))] * parts,
        cost_estimate=pl.CostEstimate(
            flops=2 * slots * rows * width, bytes_accessed=2 * rows * width, transcendentals=0
        ),
        compiler_params=pltpu.CompilerParams(vmem_limit_bytes=24 * 1024 * 1024),
        name=name,
    )(scaled, *acts)


def all_to_all(value, axis, groups):
    return lax.all_to_all(value, axis, 0, 0, tiled=True, axis_index_groups=groups)


def shards(acts, out_grads, other_sq, noise):
    dp, te = lax.axis_index("dp"), lax.axis_index("tensor")
    y, xh, c, xl, z = dp // 4, (dp // 2) % 2, dp % 2, te // NZ, te % NZ
    examples, seq, columns = acts.shape
    tokens = examples * seq
    features = out_grads.shape[2]
    rows = features // 2
    stage = lax.optimization_barrier
    z_rings = [list(range(first, first + NZ)) for first in (0, NZ)]
    chip_pairs = [list(range(first, first + 4)) for first in range(0, 4 * NY, 4)]

    flat = acts.reshape(tokens, columns)
    grads_t = out_grads.reshape(tokens, features).T
    sources = [send(grads_t, spread(0)), send(grads_t, spread(1))]

    def blocks(x):
        gram = jnp.einsum("btf,bsf->bts", x, x, preferred_element_type=F32).astype(BF)
        mid = seq // 2
        return jnp.stack([gram[:, :mid, :mid], gram[:, :mid, mid:], gram[:, mid:, mid:]])

    grams = jnp.stack([blocks(acts), blocks(out_grads)])
    grams = (grams.astype(F32) + send(grams, XLO).astype(F32)).astype(BF)
    others = jnp.sum(other_sq, axis=1)
    others = others + send(others, XLO)
    own, grams, flat, others = stage((jnp.stack(sources), grams, flat, others))

    up = send(flat[:seq], along_x(1))
    down = send(flat[seq:], along_x(-1))
    sibling = send(flat, CORE)
    fwd, bwd = [own, send(own, along_z(1))], [own, send(own, along_z(-1))]
    grams, sibling = stage((grams, sibling))
    shape = grams.shape
    grams = jnp.moveaxis(grams.reshape(shape[:3] + (NZ, -1, shape[4])), 3, 0)
    grams = all_to_all(grams, "tensor", z_rings).astype(F32).sum(axis=0)
    weight = jnp.array([1.0, 2.0, 1.0], F32)[:, None, None, None]
    total = jnp.sum(grams[0] * grams[1] * weight, axis=(0, 2, 3)) + others
    up, down, sibling, fwd[1], bwd[1], total = stage((up, down, sibling, fwd[1], bwd[1], total))

    up, down = send(up, along_x(1)), send(down, along_x(-1))
    fwd.append(send(fwd[1], along_z(1)))
    bwd.append(send(bwd[1], along_z(-1)))
    total = all_to_all(jnp.broadcast_to(total, (NZ, examples)), "tensor", z_rings).sum(axis=0)
    fwd[2], bwd[2], total = stage((fwd[2], bwd[2], total))

    fwd.append(send(fwd[2], along_z(1)))
    bwd.append(send(bwd[2], along_z(-1)))
    far = [send(fwd[2][0], along_z(2)), send(bwd[2][1], along_z(-2))]
    clip = jnp.minimum(1.0, clip_norm / jnp.sqrt(total))
    clips = all_to_all(jnp.broadcast_to(clip, (4, examples)), "dp", chip_pairs).reshape(-1)
    fwd[3], bwd[3], far, clips, up, down = stage((fwd[3], bwd[3], far, clips, up, down))
    up_sibling, down_sibling = send(up, CORE), send(down, CORE)
    pieces = [own, fwd[1], fwd[2], fwd[3], far[0], far[1], bwd[3], bwd[2], bwd[1]]
    places = jnp.stack([dp, te]).astype(jnp.int32)
    scaled = scale_grads(places, clips, pieces)

    held = [flat, sibling, up, down, up_sibling, down_sibling]
    tile = columns // 3
    far_a, far_b = product("product_far", scaled, 2, 1, held, tile, 2, BF)
    from_down, from_up = send(far_a, along_y(1)), send(far_b, along_y(-1))
    next_a, next_b, prev_a, prev_b = product("product_near", scaled, 0, 2, held, tile, 4, BF)
    next_b, prev_a = send(next_b, along_y(1)), send(prev_a, along_y(-1))
    next_a = (next_a.astype(F32) + from_down.astype(F32)).astype(BF)
    prev_b = (prev_b.astype(F32) + from_up.astype(F32)).astype(BF)
    next_a, prev_b, scaled = stage((next_a, prev_b, scaled))
    next_a, prev_b = send(next_a, along_y(1)), send(prev_b, along_y(-1))
    (mine,) = product("product_own", scaled, 3, 1, held, tile, 1, F32)

    width = features * 2 * NZ
    factor = math.sqrt(columns * 2 * NZ * width) / clip_norm
    root = math.sqrt(examples * 4 * NY)
    summed = jnp.concatenate(
        [next_a.astype(F32) + prev_a.astype(F32), next_b.astype(F32) + prev_b.astype(F32)]
    )
    return (factor * (mine + summed) + noise) / root


def solution(mesh):
    placed = (
        P("dp", None, "tensor"),
        P("dp", None, "tensor"),
        P("dp", "tensor"),
        P("dp", "tensor"),
    )
    return jax.shard_map(
        shards, mesh=mesh, in_specs=placed, out_specs=P("dp", "tensor"), check_vma=False
    )
```

```python
import math

import jax
import jax.numpy as jnp
from jax import lax
from jax.experimental import pallas as pl
from jax.experimental.pallas import tpu as pltpu
from jax.sharding import PartitionSpec as P

clip_norm = 2.5
AXES = ("dp", "tensor")
NY, NX, NZ = 4, 4, 8
OFF = (0, 1, 2, -1)
BF = jnp.bfloat16
F32 = jnp.float32


def coords(i):
    dp, te = divmod(i, 2 * NZ)
    return dp // 4, (dp // 2) % 2, dp % 2, te // NZ, te % NZ


def index(y, xh, c, xl, z):
    return ((y % NY * 2 + xh) * 2 + c) * 2 * NZ + xl * NZ + z % NZ


def perm_of(move):
    return [(i, index(*move(*coords(i)))) for i in range(NY * NX * NZ * 2)]


def along_x(step):
    def move(y, xh, c, xl, z):
        x = (xh * 2 + xl + step) % NX
        return y, x // 2, c, x % 2, z

    return perm_of(move)


def along_y(step):
    return perm_of(lambda y, xh, c, xl, z: (y + step, xh, c, xl, z))


def along_z(step):
    return perm_of(lambda y, xh, c, xl, z: (y, xh, c, xl, z + step))


def flip_z(bit):
    return perm_of(lambda y, xh, c, xl, z: (y, xh, c, xl, z ^ bit))


def spread(flip):
    def move(y, xh, c, xl, z):
        t, u = (z // 2) % 2, z % 2
        m = 2 * (xh ^ t) + (c ^ u)
        return y, t, u, xl ^ flip, z + OFF[m]

    return perm_of(move)


CORE = perm_of(lambda y, xh, c, xl, z: (y, xh, 1 - c, xl, z))
XHI = perm_of(lambda y, xh, c, xl, z: (y, 1 - xh, c, xl, z))
XLO = perm_of(lambda y, xh, c, xl, z: (y, xh, c, 1 - xl, z))


def send(value, perm):
    return lax.ppermute(value, AXES, perm)


def position(place_ref, r, f):
    dp, te = place_ref[0], place_ref[1]
    y, xh, c, xl, z = dp // 4, (dp // 2) % 2, dp % 2, te // NZ, te % NZ
    q = (z - r - 2 * xh - c + 2 * NZ) % NZ
    m = q % 4
    k = ((q + 1) // 4) % 2
    step = (2 * ((f + xl) % 2) + k - y + 4) % 4
    slot = jnp.where(step == 0, 3, jnp.where(step == 1, 0, jnp.where(step == 2, 2, 1)))
    return slot, m, 2 * (xh ^ (m // 2)) + (c ^ (m % 2))


def scale_kernel(place_ref, clip_ref, *refs):
    pieces, out_ref, held_ref, arrived = refs[:-3], refs[-3], refs[-2], refs[-1]
    half = out_ref.shape[3] // 2
    copies = [
        pltpu.make_async_copy(piece, held_ref.at[pl.ds(2 * i, 2)], arrived.at[i])
        for i, piece in enumerate(pieces)
    ]
    for copy in copies:
        copy.start()
    for i, copy in enumerate(copies):
        copy.wait()
        for f in range(2):
            slot, m, member = position(place_ref, i + (i > 3), f)
            for e in range(2):
                cols = slice(e * half, (e + 1) * half)
                out_ref[slot, m, :, cols] = (
                    clip_ref[2 * member + e] * held_ref[2 * i + f, :, cols].astype(F32)
                ).astype(BF)


def last_kernel(place_ref, clip_ref, first_ref, second_ref, _, out_ref, held_ref, done):
    half = held_ref.shape[2] // 2
    copies = []
    for f, ref in enumerate((first_ref, second_ref)):
        slot, m, member = position(place_ref, 4, f)
        for e in range(2):
            cols = slice(e * half, (e + 1) * half)
            held_ref[f, :, cols] = (
                clip_ref[2 * member + e] * ref[:, cols].astype(F32)
            ).astype(BF)
        copies.append(pltpu.make_async_copy(held_ref.at[f], out_ref.at[slot, m], done.at[f]))
        copies[-1].start()
    for copy in copies:
        copy.wait()


def scale_grads(places, clips, pieces, far):
    _, rows, tokens = pieces[0].shape
    smem = pl.BlockSpec(memory_space=pltpu.SMEM)
    vmem = pl.BlockSpec(memory_space=pltpu.VMEM)
    anywhere = pl.BlockSpec(memory_space=pl.ANY)
    shape = jax.ShapeDtypeStruct((4, 4, rows, tokens), BF)
    cost = pl.CostEstimate(
        flops=16 * rows * tokens, bytes_accessed=rows * tokens, transcendentals=0
    )
    params = pltpu.CompilerParams(vmem_limit_bytes=24 * 1024 * 1024)
    most = pl.pallas_call(
        scale_kernel,
        out_shape=shape,
        in_specs=[smem, smem] + [anywhere] * len(pieces),
        out_specs=vmem,
        scratch_shapes=[
            pltpu.VMEM((2 * len(pieces), rows, tokens), BF),
            pltpu.SemaphoreType.DMA((len(pieces),)),
        ],
        cost_estimate=cost,
        compiler_params=params,
        name="scale_grads",
    )(places, clips, *pieces)
    return pl.pallas_call(
        last_kernel,
        out_shape=shape,
        in_specs=[smem, smem, vmem, vmem, anywhere],
        out_specs=anywhere,
        scratch_shapes=[pltpu.VMEM((2, rows, tokens), BF), pltpu.SemaphoreType.DMA((2,))],
        input_output_aliases={4: 0},
        cost_estimate=cost,
        compiler_params=params,
        name="scale_last",
    )(places, clips, *far, most)


def product_kernel(s_ref, *refs):
    acts, outs = refs[:6], refs[6:]
    slots, _, rows, tokens = s_ref.shape
    total = None
    first = 0
    for a_ref in acts:
        count = a_ref.shape[0]
        m, start = first // tokens, first % tokens
        left = s_ref[:, m, :, start : start + count].reshape(slots * rows, count)
        part = jnp.dot(left, a_ref[...], preferred_element_type=F32)
        total = part if total is None else total + part
        first += count
    first = 0
    for out_ref in outs:
        count = out_ref.shape[0]
        out_ref[...] = total[first : first + count].astype(out_ref.dtype)
        first += count


def product(name, scaled, first, slots, acts, tile, parts, dtype):
    _, quarters, rows, tokens = scaled.shape
    width = acts[0].shape[1]
    count = slots * rows // parts
    return pl.pallas_call(
        product_kernel,
        out_shape=[jax.ShapeDtypeStruct((count, width), dtype)] * parts,
        grid=(width // tile,),
        in_specs=[
            pl.BlockSpec((slots, quarters, rows, tokens), lambda j: (first // slots, 0, 0, 0))
        ]
        + [pl.BlockSpec((a.shape[0], tile), lambda j: (0, j)) for a in acts],
        out_specs=[pl.BlockSpec((count, tile), lambda j: (0, j))] * parts,
        cost_estimate=pl.CostEstimate(
            flops=2 * slots * rows * width, bytes_accessed=2 * rows * width, transcendentals=0
        ),
        compiler_params=pltpu.CompilerParams(vmem_limit_bytes=24 * 1024 * 1024),
        name=name,
    )(scaled, *acts)


def all_to_all(value, axis, groups):
    return lax.all_to_all(value, axis, 0, 0, tiled=True, axis_index_groups=groups)


def shards(acts, out_grads, other_sq, noise):
    dp, te = lax.axis_index("dp"), lax.axis_index("tensor")
    y, xh, c, xl, z = dp // 4, (dp // 2) % 2, dp % 2, te // NZ, te % NZ
    examples, seq, columns = acts.shape
    tokens = examples * seq
    features = out_grads.shape[2]
    rows = features // 2
    stage = lax.optimization_barrier
    z_rings = [list(range(first, first + NZ)) for first in (0, NZ)]
    chip_pairs = [list(range(first, first + 4)) for first in range(0, 4 * NY, 4)]

    flat = acts.reshape(tokens, columns)
    grads_t = out_grads.reshape(tokens, features).T
    sources = [send(grads_t, spread(0)), send(grads_t, spread(1))]

    def blocks(x):
        gram = jnp.einsum("btf,bsf->bts", x, x, preferred_element_type=F32).astype(BF)
        mid = seq // 2
        return jnp.stack([gram[:, :mid, :mid], gram[:, :mid, mid:], gram[:, mid:, mid:]])

    grams = jnp.stack([blocks(acts), blocks(out_grads)])
    grams = (grams.astype(F32) + send(grams, XLO).astype(F32)).astype(BF)
    others = jnp.sum(other_sq, axis=1)
    others = others + send(others, XLO)
    sources, grams, flat, others = stage((sources, grams, flat, others))

    up = send(flat[:seq], along_x(1))
    down = send(flat[seq:], along_x(-1))
    own = jnp.stack(sources)
    fwd, bwd = [own, send(own, along_z(1))], [own, send(own, along_z(-1))]
    shape = grams.shape
    grams = jnp.moveaxis(grams.reshape(shape[:3] + (NZ, -1, shape[4])), 3, 0)
    grams = all_to_all(grams, "tensor", z_rings).astype(F32).sum(axis=0)
    weight = jnp.array([1.0, 2.0, 1.0], F32)[:, None, None, None]
    total = jnp.sum(grams[0] * grams[1] * weight, axis=(0, 2, 3)) + others
    up, down, fwd[1], bwd[1], total = stage((up, down, fwd[1], bwd[1], total))

    up, down = send(up, along_x(1)), send(down, along_x(-1))
    fwd.append(send(fwd[1], along_z(1)))
    bwd.append(send(bwd[1], along_z(-1)))
    sibling = send(flat, CORE)
    total = all_to_all(jnp.broadcast_to(total, (NZ, examples)), "tensor", z_rings).sum(axis=0)
    fwd[2], bwd[2], total = stage((fwd[2], bwd[2], total))

    fwd.append(send(fwd[2], along_z(1)))
    bwd.append(send(bwd[2], along_z(-1)))
    clip = jnp.minimum(1.0, clip_norm / jnp.sqrt(total))
    clips = all_to_all(jnp.broadcast_to(clip, (4, examples)), "dp", chip_pairs).reshape(-1)
    fwd[3], bwd[3], clips, up, down = stage((fwd[3], bwd[3], clips, up, down))

    far = [send(fwd[3][0], along_z(1)), send(bwd[3][1], along_z(-1))]
    up_sibling, down_sibling = send(up, CORE), send(down, CORE)
    pieces = [own, fwd[1], fwd[2], fwd[3], bwd[3], bwd[2], bwd[1]]
    places = jnp.stack([dp, te]).astype(jnp.int32)
    scaled = scale_grads(places, clips, pieces, far)

    held = [flat, sibling, up, down, up_sibling, down_sibling]
    tile = columns // 3
    far_a, far_b = product("product_far", scaled, 2, 1, held, tile, 2, BF)
    from_down, from_up = send(far_a, along_y(1)), send(far_b, along_y(-1))
    next_a, next_b, prev_a, prev_b = product("product_near", scaled, 0, 2, held, tile, 4, BF)
    next_b, prev_a = send(next_b, along_y(1)), send(prev_a, along_y(-1))
    next_a = (next_a.astype(F32) + from_down.astype(F32)).astype(BF)
    prev_b = (prev_b.astype(F32) + from_up.astype(F32)).astype(BF)
    next_a, prev_b, scaled = stage((next_a, prev_b, scaled))
    next_a, prev_b = send(next_a, along_y(1)), send(prev_b, along_y(-1))
    (mine,) = product("product_own", scaled, 3, 1, held, tile, 1, F32)

    width = features * 2 * NZ
    factor = math.sqrt(columns * 2 * NZ * width) / clip_norm
    root = math.sqrt(examples * 4 * NY)
    summed = jnp.concatenate(
        [next_a.astype(F32) + prev_a.astype(F32), next_b.astype(F32) + prev_b.astype(F32)]
    )
    return (factor * (mine + summed) + noise) / root


def solution(mesh):
    placed = (
        P("dp", None, "tensor"),
        P("dp", None, "tensor"),
        P("dp", "tensor"),
        P("dp", "tensor"),
    )
    return jax.shard_map(
        shards, mesh=mesh, in_specs=placed, out_specs=P("dp", "tensor"), check_vma=False
    )
```

```python
import functools
import math

import jax
import jax.numpy as jnp
from jax import lax
from jax.experimental import pallas as pl
from jax.experimental.pallas import tpu as pltpu
from jax.sharding import PartitionSpec as P

clip_norm = 2.5
AXES = ("dp", "tensor")
NY, NX, NZ = 4, 4, 8
OFF = (0, 1, 2, -1)
BF = jnp.bfloat16
F32 = jnp.float32


def coords(i):
    dp, te = divmod(i, 2 * NZ)
    return dp // 4, (dp // 2) % 2, dp % 2, te // NZ, te % NZ


def index(y, xh, c, xl, z):
    return ((y % NY * 2 + xh) * 2 + c) * 2 * NZ + xl * NZ + z % NZ


def perm_of(move):
    return [(i, index(*move(*coords(i)))) for i in range(NY * NX * NZ * 2)]


def along_x(step):
    def move(y, xh, c, xl, z):
        x = (xh * 2 + xl + step) % NX
        return y, x // 2, c, x % 2, z

    return perm_of(move)


def along_y(step):
    return perm_of(lambda y, xh, c, xl, z: (y + step, xh, c, xl, z))


def along_z(step):
    return perm_of(lambda y, xh, c, xl, z: (y, xh, c, xl, z + step))


def flip_z(bit):
    return perm_of(lambda y, xh, c, xl, z: (y, xh, c, xl, z ^ bit))


def spread(flip):
    def move(y, xh, c, xl, z):
        t, u = (z // 2) % 2, z % 2
        m = 2 * (xh ^ t) + (c ^ u)
        return y, t, u, xl ^ flip, z + OFF[m]

    return perm_of(move)


CORE = perm_of(lambda y, xh, c, xl, z: (y, xh, 1 - c, xl, z))
XHI = perm_of(lambda y, xh, c, xl, z: (y, 1 - xh, c, xl, z))
XLO = perm_of(lambda y, xh, c, xl, z: (y, xh, c, 1 - xl, z))


def send(value, perm):
    return lax.ppermute(value, AXES, perm)


def position(place_ref, r, f):
    dp, te = place_ref[0], place_ref[1]
    y, xh, c, xl, z = dp // 4, (dp // 2) % 2, dp % 2, te // NZ, te % NZ
    q = (z - r - 2 * xh - c + 2 * NZ) % NZ
    m = q % 4
    k = ((q + 1) // 4) % 2
    step = (2 * ((f + xl) % 2) + k - y + 4) % 4
    slot = jnp.where(step == 0, 3, jnp.where(step == 1, 0, jnp.where(step == 2, 2, 1)))
    return slot, m, 2 * (xh ^ (m // 2)) + (c ^ (m % 2))


NEAR = (3, 4)


def scale_kernel(place_ref, clip_ref, *refs):
    pieces, out_ref, held_ref, arrived = refs[:-3], refs[-3], refs[-2], refs[-1]
    half = out_ref.shape[3] // 2
    copies = {}
    for i, piece in enumerate(pieces):
        if i not in NEAR:
            place = held_ref.at[pl.ds(2 * len(copies), 2)]
            copies[i] = (pltpu.make_async_copy(piece, place, arrived.at[i]), place)
            copies[i][0].start()
    for i, piece in enumerate(pieces):
        blocks = piece
        if i in copies:
            copies[i][0].wait()
            blocks = copies[i][1]
        for f in range(2):
            slot, m, member = position(place_ref, i + (i > 3), f)
            for e in range(2):
                cols = slice(e * half, (e + 1) * half)
                out_ref[slot, m, :, cols] = (
                    clip_ref[member, e] * blocks[f, :, cols].astype(F32)
                ).astype(BF)


def last_kernel(place_ref, clip_ref, first_ref, second_ref, _, out_ref, held_ref, done):
    half = held_ref.shape[2] // 2
    copies = []
    for f, ref in enumerate((first_ref, second_ref)):
        slot, m, member = position(place_ref, 4, f)
        for e in range(2):
            cols = slice(e * half, (e + 1) * half)
            held_ref[f, :, cols] = (
                clip_ref[member, e] * ref[:, cols].astype(F32)
            ).astype(BF)
        copies.append(pltpu.make_async_copy(held_ref.at[f], out_ref.at[slot, m], done.at[f]))
        copies[-1].start()
    for copy in copies:
        copy.wait()


def scale_grads(places, clips, pieces, far):
    _, rows, tokens = pieces[0].shape
    smem = pl.BlockSpec(memory_space=pltpu.SMEM)
    vmem = pl.BlockSpec(memory_space=pltpu.VMEM)
    anywhere = pl.BlockSpec(memory_space=pl.ANY)
    shape = jax.ShapeDtypeStruct((4, 4, rows, tokens), BF)
    cost = pl.CostEstimate(
        flops=16 * rows * tokens, bytes_accessed=rows * tokens, transcendentals=0
    )
    params = pltpu.CompilerParams(vmem_limit_bytes=24 * 1024 * 1024)
    most = pl.pallas_call(
        scale_kernel,
        out_shape=shape,
        in_specs=[smem, smem]
        + [vmem if i in NEAR else anywhere for i in range(len(pieces))],
        out_specs=vmem,
        scratch_shapes=[
            pltpu.VMEM((2 * (len(pieces) - len(NEAR)), rows, tokens), BF),
            pltpu.SemaphoreType.DMA((len(pieces),)),
        ],
        cost_estimate=cost,
        compiler_params=params,
        name="scale_grads",
    )(places, clips, *pieces)
    return pl.pallas_call(
        last_kernel,
        out_shape=shape,
        in_specs=[smem, smem, vmem, vmem, anywhere],
        out_specs=anywhere,
        scratch_shapes=[pltpu.VMEM((2, rows, tokens), BF), pltpu.SemaphoreType.DMA((2,))],
        input_output_aliases={4: 0},
        cost_estimate=cost,
        compiler_params=params,
        name="scale_last",
    )(places, clips, *far, most)


def product_kernel(scale, s_ref, *refs):
    acts, outs = refs[:6], refs[6:]
    slots, _, rows, tokens = s_ref.shape
    total = None
    first = 0
    for a_ref in acts:
        count = a_ref.shape[0]
        m, start = first // tokens, first % tokens
        left = s_ref[:, m, :, start : start + count].reshape(slots * rows, count)
        part = jnp.dot(left, a_ref[...], preferred_element_type=F32)
        total = part if total is None else total + part
        first += count
    if scale is not None:
        noise_ref, outs = outs[0], outs[1:]
        total = (scale[0] * total + noise_ref[...]) / scale[1]
    first = 0
    for out_ref in outs:
        count = out_ref.shape[0]
        out_ref[...] = total[first : first + count].astype(out_ref.dtype)
        first += count


def product(name, scaled, first, slots, acts, tile, parts, dtype, noise=(), scale=None):
    _, quarters, rows, tokens = scaled.shape
    width = acts[0].shape[1]
    count = slots * rows // parts
    return pl.pallas_call(
        functools.partial(product_kernel, scale),
        out_shape=[jax.ShapeDtypeStruct((count, width), dtype)] * parts,
        grid=(width // tile,),
        in_specs=[
            pl.BlockSpec((slots, quarters, rows, tokens), lambda j: (first // slots, 0, 0, 0))
        ]
        + [pl.BlockSpec((a.shape[0], tile), lambda j: (0, j)) for a in [*acts, *noise]],
        out_specs=[pl.BlockSpec((count, tile), lambda j: (0, j))] * parts,
        cost_estimate=pl.CostEstimate(
            flops=2 * slots * rows * width, bytes_accessed=2 * rows * width, transcendentals=0
        ),
        compiler_params=pltpu.CompilerParams(vmem_limit_bytes=24 * 1024 * 1024),
        name=name,
    )(scaled, *acts, *noise)


def all_to_all(value, axis, groups):
    return lax.all_to_all(value, axis, 0, 0, tiled=True, axis_index_groups=groups)


def shards(acts, out_grads, other_sq, noise):
    dp, te = lax.axis_index("dp"), lax.axis_index("tensor")
    y, xh, c, xl, z = dp // 4, (dp // 2) % 2, dp % 2, te // NZ, te % NZ
    examples, seq, columns = acts.shape
    tokens = examples * seq
    features = out_grads.shape[2]
    rows = features // 2
    stage = lax.optimization_barrier
    z_rings = [list(range(first, first + NZ)) for first in (0, NZ)]
    chip_pairs = [list(range(first, first + 4)) for first in range(0, 4 * NY, 4)]

    flat = acts.reshape(tokens, columns)
    grads_t = out_grads.reshape(tokens, features).T
    sources = [send(grads_t, spread(0)), send(grads_t, spread(1))]

    def blocks(x):
        gram = jnp.einsum("btf,bsf->bts", x, x, preferred_element_type=F32).astype(BF)
        mid = seq // 2
        return jnp.stack([gram[:, :mid, :mid], gram[:, :mid, mid:], gram[:, mid:, mid:]])

    grams = jnp.stack([blocks(acts), blocks(out_grads)])
    grams = (grams.astype(F32) + send(grams, XLO).astype(F32)).astype(BF)
    others = jnp.sum(other_sq, axis=1)
    others = others + send(others, XLO)
    sources, grams, flat, others = stage((sources, grams, flat, others))

    up = send(flat[:seq], along_x(1))
    down = send(flat[seq:], along_x(-1))
    own = jnp.stack(sources)
    fwd, bwd = [own, send(own, along_z(1))], [own, send(own, along_z(-1))]
    shape = grams.shape
    grams = jnp.moveaxis(grams.reshape(shape[:3] + (NZ, -1, shape[4])), 3, 0)
    grams = all_to_all(grams, "tensor", z_rings).astype(F32).sum(axis=0)
    weight = jnp.array([1.0, 2.0, 1.0], F32)[:, None, None, None]
    total = jnp.sum(grams[0] * grams[1] * weight, axis=(0, 2, 3)) + others
    up, down, fwd[1], bwd[1], total = stage((up, down, fwd[1], bwd[1], total))

    up, down = send(up, along_x(1)), send(down, along_x(-1))
    fwd.append(send(fwd[1], along_z(1)))
    bwd.append(send(bwd[1], along_z(-1)))
    sibling = send(flat, CORE)
    total = all_to_all(jnp.broadcast_to(total, (NZ, examples)), "tensor", z_rings).sum(axis=0)
    fwd[2], bwd[2], total = stage((fwd[2], bwd[2], total))

    fwd.append(send(fwd[2], along_z(1)))
    bwd.append(send(bwd[2], along_z(-1)))
    clip = jnp.minimum(1.0, clip_norm / jnp.sqrt(total))
    clips = all_to_all(jnp.broadcast_to(clip, (4, examples)), "dp", chip_pairs)
    fwd[3], bwd[3], clips, up, down = stage((fwd[3], bwd[3], clips, up, down))

    far = [send(fwd[3][0], along_z(1)), send(bwd[3][1], along_z(-1))]
    up_sibling, down_sibling = send(up, CORE), send(down, CORE)
    pieces = [own, fwd[1], fwd[2], fwd[3], bwd[3], bwd[2], bwd[1]]
    places = jnp.stack([dp, te]).astype(jnp.int32)
    scaled = scale_grads(places, clips, pieces, far)

    held = [flat, sibling, up, down, up_sibling, down_sibling]
    tile = columns // 3
    far_a, far_b = product("product_far", scaled, 2, 1, held, tile, 2, BF)
    from_down, from_up = send(far_a, along_y(1)), send(far_b, along_y(-1))
    next_a, next_b, prev_a, prev_b = product("product_near", scaled, 0, 2, held, tile, 4, BF)
    next_b, prev_a = send(next_b, along_y(1)), send(prev_a, along_y(-1))
    next_a = (next_a.astype(F32) + from_down.astype(F32)).astype(BF)
    prev_b = (prev_b.astype(F32) + from_up.astype(F32)).astype(BF)
    next_a, prev_b, scaled = stage((next_a, prev_b, scaled))
    next_a, prev_b = send(next_a, along_y(1)), send(prev_b, along_y(-1))
    width = features * 2 * NZ
    factor = math.sqrt(columns * 2 * NZ * width) / clip_norm
    root = math.sqrt(examples * 4 * NY)
    (mine,) = product(
        "product_own", scaled, 3, 1, held, tile, 1, F32, [noise], (factor, root)
    )
    summed = jnp.concatenate(
        [next_a.astype(F32) + prev_a.astype(F32), next_b.astype(F32) + prev_b.astype(F32)]
    )
    return mine + (factor / root) * summed


def solution(mesh):
    placed = (
        P("dp", None, "tensor"),
        P("dp", None, "tensor"),
        P("dp", "tensor"),
        P("dp", "tensor"),
    )
    return jax.shard_map(
        shards, mesh=mesh, in_specs=placed, out_specs=P("dp", "tensor"), check_vma=False
    )
```

```python
import functools
import math

import jax
import jax.numpy as jnp
from jax import lax
from jax.experimental import pallas as pl
from jax.experimental.pallas import tpu as pltpu
from jax.sharding import PartitionSpec as P

clip_norm = 2.5
AXES = ("dp", "tensor")
NY, NX, NZ = 4, 4, 8
OFF = (0, 1, 2, -1)
BF = jnp.bfloat16
F32 = jnp.float32


def coords(i):
    dp, te = divmod(i, 2 * NZ)
    return dp // 4, (dp // 2) % 2, dp % 2, te // NZ, te % NZ


def index(y, xh, c, xl, z):
    return ((y % NY * 2 + xh) * 2 + c) * 2 * NZ + xl * NZ + z % NZ


def perm_of(move):
    return [(i, index(*move(*coords(i)))) for i in range(NY * NX * NZ * 2)]


def along_x(step):
    def move(y, xh, c, xl, z):
        x = (xh * 2 + xl + step) % NX
        return y, x // 2, c, x % 2, z

    return perm_of(move)


def along_y(step):
    return perm_of(lambda y, xh, c, xl, z: (y + step, xh, c, xl, z))


def along_z(step):
    return perm_of(lambda y, xh, c, xl, z: (y, xh, c, xl, z + step))


def flip_z(bit):
    return perm_of(lambda y, xh, c, xl, z: (y, xh, c, xl, z ^ bit))


def spread(flip):
    def move(y, xh, c, xl, z):
        t, u = (z // 2) % 2, z % 2
        m = 2 * (xh ^ t) + (c ^ u)
        return y, t, u, xl ^ flip, z + OFF[m]

    return perm_of(move)


APART = perm_of(lambda y, xh, c, xl, z: (y, xh, c, xl, z + 1 - 2 * c))
CORE = perm_of(lambda y, xh, c, xl, z: (y, xh, 1 - c, xl, z))
XHI = perm_of(lambda y, xh, c, xl, z: (y, 1 - xh, c, xl, z))
XLO = perm_of(lambda y, xh, c, xl, z: (y, xh, c, 1 - xl, z))


def send(value, perm):
    return lax.ppermute(value, AXES, perm)


def position(place_ref, r, f):
    dp, te = place_ref[0], place_ref[1]
    y, xh, c, xl, z = dp // 4, (dp // 2) % 2, dp % 2, te // NZ, te % NZ
    q = (z - r - 2 * xh - c + 2 * NZ) % NZ
    m = q % 4
    k = ((q + 1) // 4) % 2
    step = (2 * ((f + xl) % 2) + k - y + 4) % 4
    slot = jnp.where(step == 0, 3, jnp.where(step == 1, 0, jnp.where(step == 2, 2, 1)))
    return slot, m, 2 * (xh ^ (m // 2)) + (c ^ (m % 2))


NEAR = (3, 4)


def scale_kernel(place_ref, clip_ref, *refs):
    pieces, out_ref, held_ref, arrived = refs[:-3], refs[-3], refs[-2], refs[-1]
    half = out_ref.shape[3] // 2
    copies = {}
    for i, piece in enumerate(pieces):
        if i not in NEAR:
            place = held_ref.at[pl.ds(2 * len(copies), 2)]
            copies[i] = (pltpu.make_async_copy(piece, place, arrived.at[i]), place)
            copies[i][0].start()
    for i, piece in enumerate(pieces):
        blocks = piece
        if i in copies:
            copies[i][0].wait()
            blocks = copies[i][1]
        for f in range(2):
            slot, m, member = position(place_ref, i + (i > 3), f)
            for e in range(2):
                cols = slice(e * half, (e + 1) * half)
                out_ref[slot, m, :, cols] = (
                    clip_ref[member, e] * blocks[f, :, cols].astype(F32)
                ).astype(BF)


def last_kernel(place_ref, clip_ref, far_ref, _, out_ref, held_ref, done):
    half = held_ref.shape[2] // 2
    copies = []
    for f in range(2):
        slot, m, member = position(place_ref, 4, f)
        for e in range(2):
            cols = slice(e * half, (e + 1) * half)
            held_ref[f, :, cols] = (
                clip_ref[member, e] * far_ref[f, :, cols].astype(F32)
            ).astype(BF)
        copies.append(pltpu.make_async_copy(held_ref.at[f], out_ref.at[slot, m], done.at[f]))
        copies[-1].start()
    for copy in copies:
        copy.wait()


def scale_grads(places, clips, pieces, far):
    _, rows, tokens = pieces[0].shape
    smem = pl.BlockSpec(memory_space=pltpu.SMEM)
    vmem = pl.BlockSpec(memory_space=pltpu.VMEM)
    anywhere = pl.BlockSpec(memory_space=pl.ANY)
    shape = jax.ShapeDtypeStruct((4, 4, rows, tokens), BF)
    cost = pl.CostEstimate(
        flops=16 * rows * tokens, bytes_accessed=rows * tokens, transcendentals=0
    )
    params = pltpu.CompilerParams(vmem_limit_bytes=24 * 1024 * 1024)
    most = pl.pallas_call(
        scale_kernel,
        out_shape=shape,
        in_specs=[smem, smem]
        + [vmem if i in NEAR else anywhere for i in range(len(pieces))],
        out_specs=vmem,
        scratch_shapes=[
            pltpu.VMEM((2 * (len(pieces) - len(NEAR)), rows, tokens), BF),
            pltpu.SemaphoreType.DMA((len(pieces),)),
        ],
        cost_estimate=cost,
        compiler_params=params,
        name="scale_grads",
    )(places, clips, *pieces)
    return pl.pallas_call(
        last_kernel,
        out_shape=shape,
        in_specs=[smem, smem, vmem, anywhere],
        out_specs=anywhere,
        scratch_shapes=[pltpu.VMEM((2, rows, tokens), BF), pltpu.SemaphoreType.DMA((2,))],
        input_output_aliases={3: 0},
        cost_estimate=cost,
        compiler_params=params,
        name="scale_last",
    )(places, clips, far, most)


def product_kernel(scale, s_ref, *refs):
    acts, outs = refs[:6], refs[6:]
    slots, _, rows, tokens = s_ref.shape
    total = None
    first = 0
    for a_ref in acts:
        count = a_ref.shape[0]
        m, start = first // tokens, first % tokens
        left = s_ref[:, m, :, start : start + count].reshape(slots * rows, count)
        part = jnp.dot(left, a_ref[...], preferred_element_type=F32)
        total = part if total is None else total + part
        first += count
    if scale is not None:
        noise_ref, outs = outs[0], outs[1:]
        total = (scale[0] * total + noise_ref[...]) / scale[1]
    first = 0
    for out_ref in outs:
        count = out_ref.shape[0]
        out_ref[...] = total[first : first + count].astype(out_ref.dtype)
        first += count


def product(name, scaled, first, slots, acts, tile, parts, dtype, noise=(), scale=None):
    _, quarters, rows, tokens = scaled.shape
    width = acts[0].shape[1]
    count = slots * rows // parts
    return pl.pallas_call(
        functools.partial(product_kernel, scale),
        out_shape=[jax.ShapeDtypeStruct((count, width), dtype)] * parts,
        grid=(width // tile,),
        in_specs=[
            pl.BlockSpec((slots, quarters, rows, tokens), lambda j: (first // slots, 0, 0, 0))
        ]
        + [pl.BlockSpec((a.shape[0], tile), lambda j: (0, j)) for a in [*acts, *noise]],
        out_specs=[pl.BlockSpec((count, tile), lambda j: (0, j))] * parts,
        cost_estimate=pl.CostEstimate(
            flops=2 * slots * rows * width, bytes_accessed=2 * rows * width, transcendentals=0
        ),
        compiler_params=pltpu.CompilerParams(vmem_limit_bytes=24 * 1024 * 1024),
        name=name,
    )(scaled, *acts, *noise)


def all_to_all(value, axis, groups):
    return lax.all_to_all(value, axis, 0, 0, tiled=True, axis_index_groups=groups)


def shards(acts, out_grads, other_sq, noise):
    dp, te = lax.axis_index("dp"), lax.axis_index("tensor")
    y, xh, c, xl, z = dp // 4, (dp // 2) % 2, dp % 2, te // NZ, te % NZ
    examples, seq, columns = acts.shape
    tokens = examples * seq
    features = out_grads.shape[2]
    rows = features // 2
    stage = lax.optimization_barrier
    z_rings = [list(range(first, first + NZ)) for first in (0, NZ)]
    chip_pairs = [list(range(first, first + 4)) for first in range(0, 4 * NY, 4)]

    flat = acts.reshape(tokens, columns)
    grads_t = out_grads.reshape(tokens, features).T
    sources = [send(grads_t, spread(0)), send(grads_t, spread(1))]

    def blocks(x):
        gram = jnp.einsum("btf,bsf->bts", x, x, preferred_element_type=F32).astype(BF)
        mid = seq // 2
        return jnp.stack([gram[:, :mid, :mid], gram[:, :mid, mid:], gram[:, mid:, mid:]])

    grams = jnp.stack([blocks(acts), blocks(out_grads)])
    grams = (grams.astype(F32) + send(grams, XLO).astype(F32)).astype(BF)
    others = jnp.sum(other_sq, axis=1)
    others = others + send(others, XLO)
    sources, grams, flat, others = stage((sources, grams, flat, others))

    up = send(flat[:seq], along_x(1))
    down = send(flat[seq:], along_x(-1))
    own = jnp.stack(sources)
    fwd, bwd = [own, send(own, along_z(1))], [own, send(own, along_z(-1))]
    shape = grams.shape
    grams = jnp.moveaxis(grams.reshape(shape[:3] + (NZ, -1, shape[4])), 3, 0)
    grams = all_to_all(grams, "tensor", z_rings).astype(F32).sum(axis=0)
    weight = jnp.array([1.0, 2.0, 1.0], F32)[:, None, None, None]
    total = jnp.sum(grams[0] * grams[1] * weight, axis=(0, 2, 3)) + others
    up, down, fwd[1], bwd[1], total = stage((up, down, fwd[1], bwd[1], total))

    up, down = send(up, along_x(1)), send(down, along_x(-1))
    fwd.append(send(fwd[1], along_z(1)))
    bwd.append(send(bwd[1], along_z(-1)))
    sibling = send(flat, CORE)
    total = all_to_all(jnp.broadcast_to(total, (NZ, examples)), "tensor", z_rings).sum(axis=0)
    fwd[2], bwd[2], total = stage((fwd[2], bwd[2], total))

    fwd.append(send(fwd[2], along_z(1)))
    bwd.append(send(bwd[2], along_z(-1)))
    clip = jnp.minimum(1.0, clip_norm / jnp.sqrt(total))
    clips = all_to_all(jnp.broadcast_to(clip, (4, examples)), "dp", chip_pairs)
    fwd[3], bwd[3], clips, up, down = stage((fwd[3], bwd[3], clips, up, down))

    far = send(jnp.where(c == 0, fwd[3], bwd[3]), APART)
    up_sibling, down_sibling = send(up, CORE), send(down, CORE)
    pieces = [own, fwd[1], fwd[2], fwd[3], bwd[3], bwd[2], bwd[1]]
    places = jnp.stack([dp, te]).astype(jnp.int32)
    scaled = scale_grads(places, clips, pieces, far)

    held = [flat, sibling, up, down, up_sibling, down_sibling]
    tile = columns // 3
    far_a, far_b = product("product_far", scaled, 2, 1, held, tile, 2, BF)
    from_down, from_up = send(far_a, along_y(1)), send(far_b, along_y(-1))
    next_a, next_b, prev_a, prev_b = product("product_near", scaled, 0, 2, held, tile, 4, BF)
    next_b, prev_a = send(next_b, along_y(1)), send(prev_a, along_y(-1))
    next_a = (next_a.astype(F32) + from_down.astype(F32)).astype(BF)
    prev_b = (prev_b.astype(F32) + from_up.astype(F32)).astype(BF)
    next_a, prev_b, scaled = stage((next_a, prev_b, scaled))
    next_a, prev_b = send(next_a, along_y(1)), send(prev_b, along_y(-1))
    width = features * 2 * NZ
    factor = math.sqrt(columns * 2 * NZ * width) / clip_norm
    root = math.sqrt(examples * 4 * NY)
    (mine,) = product(
        "product_own", scaled, 3, 1, held, tile, 1, F32, [noise], (factor, root)
    )
    summed = jnp.concatenate(
        [next_a.astype(F32) + prev_a.astype(F32), next_b.astype(F32) + prev_b.astype(F32)]
    )
    return mine + (factor / root) * summed


def solution(mesh):
    placed = (
        P("dp", None, "tensor"),
        P("dp", None, "tensor"),
        P("dp", "tensor"),
        P("dp", "tensor"),
    )
    return jax.shard_map(
        shards, mesh=mesh, in_specs=placed, out_specs=P("dp", "tensor"), check_vma=False
    )
```
